128 devices in a mesh: mod: 2 (over x_hi), batch: 64 (over y, z, x_lo, core).
Axes of the slice: x: 4 (x_hi: 2, x_lo: 2; x = x_hi * 2 + x_lo), y: 4, z: 4, core: 2. Of those that a mesh axis runs over, the one named last changes fastest.
Arguments:
- hidden: bfloat16 [448, 2, 128, 768], P('batch', 'mod'), may hold values from -6 to 6
- text_counts: int32 [448], P('batch'), may hold values from 32 to 128, as said below
- region_counts: int32 [448], P('batch'), may hold values from 50 to 100, as said below
- qkv_weight: bfloat16 [1, 768, 2304], replicated, may hold values from -0.21875 to 0.21875
- qv_bias: bfloat16 [1, 1536], replicated, may hold values from -3 to 3
- out_weight: bfloat16 [1, 768, 768], replicated, may hold values from -1.75 to 1.75
- out_bias: bfloat16 [1, 768], replicated, may hold values from -2 to 2
- norm1_gain: bfloat16 [1, 768], replicated, may hold values from 0.5 to 1.5
- norm1_bias: bfloat16 [1, 768], replicated, may hold values from -2 to 2
- up_weight: bfloat16 [1, 768, 3072], replicated, may hold values from -0.21875 to 0.21875
- up_bias: bfloat16 [1, 3072], replicated, may hold values from -3 to 3
- down_weight: bfloat16 [1, 3072, 768], replicated, may hold values from -0.109375 to 0.109375
- down_bias: bfloat16 [1, 768], replicated, may hold values from -2 to 2
- norm2_gain: bfloat16 [1, 768], replicated, may hold values from 0.5 to 1.5
- norm2_bias: bfloat16 [1, 768], replicated, may hold values from -2 to 2
- out_grad: bfloat16 [448, 2, 128, 768], P('batch', 'mod'), may hold values from -6 to 6
Outputs:
- layer_out: bfloat16 [448, 2, 128, 768], P('batch', 'mod')
- input_grad: bfloat16 [448, 2, 128, 768], P('batch', 'mod')
- grad_qkv_weight: float32 [1, 768, 2304], replicated
- grad_qv_bias: float32 [1, 1536], replicated
- grad_out_weight: float32 [1, 768, 768], replicated
- grad_out_bias: float32 [1, 768], replicated
- grad_norm1_gain: float32 [1, 768], replicated
- grad_norm1_bias: float32 [1, 768], replicated
- grad_up_weight: float32 [1, 768, 3072], replicated
- grad_up_bias: float32 [1, 3072], replicated
- grad_down_weight: float32 [1, 3072, 768], replicated
- grad_down_bias: float32 [1, 768], replicated
- grad_norm2_gain: float32 [1, 768], replicated
- grad_norm2_bias: float32 [1, 768], replicated
The draws below stay inside these ranges and needn't reach their ends.
Inputs may be any that keep to these rules, and one draw needn't show every extreme that they name: `text_counts`: valid caption tokens of each pair; they fill the first slots of its 128 text slots. `region_counts`: valid image regions of each pair; they fill the first slots of its 128 region slots.
All inputs are finite; a program needn't handle non-finite values.
Results may differ from the reference program's by a relative error of at most 0.014.
Values may be sent and summed in bfloat16 or wider, within the bound.
A program may use at most 256 MiB of HBM per device.

```python
from functools import partial
import jax
import jax.numpy as jnp
from jax import lax

D = 768
HEADS = 12
HEAD_DIM = 64
FF = 3072
SLOTS = 128
REGIONS = 100
LAYERS = 1
PAIRS = 448
MODS = 2


def draw_text_counts(key, part):
    key = jax.random.fold_in(key, 7)
    least = max(SLOTS // 4, 1)
    counts = jax.random.randint(key, (PAIRS,), least, SLOTS + 1, dtype=jnp.int32)
    chosen = jax.random.permutation(jax.random.fold_in(key, 1), PAIRS)
    counts = counts.at[chosen[0]].set(SLOTS)
    return counts.at[chosen[1]].set(least).astype(jnp.int32)


def draw_region_counts(key, part):
    key = jax.random.fold_in(key, 9)
    least = max(REGIONS // 2, 1)
    counts = jax.random.randint(key, (PAIRS,), least, REGIONS + 1, dtype=jnp.int32)
    chosen = jax.random.permutation(jax.random.fold_in(key, 1), PAIRS)
    counts = counts.at[chosen[0]].set(REGIONS)
    return counts.at[chosen[1]].set(least).astype(jnp.int32)


def shard_levels(own_key, extent, shards, smallest, top_value):
    level, own = 1.0, jax.random.fold_in(own_key, 6)
    for position, blocks in shards:
        steps = jnp.exp(jax.random.uniform(jax.random.fold_in(own, position), (blocks,), jnp.float32, smallest / len(shards), top_value / len(shards)))
        level = level * jnp.repeat(steps, extent[position] // blocks).reshape([-1 if axis == position else 1 for axis in range(len(extent))])
    return level


def normal_values(own_key, dims, width, bound, split=(), held_as=jnp.bfloat16):
    array = width * jax.random.normal(own_key, dims, jnp.float32)
    if split:
        array = array * shard_levels(own_key, dims, split, -0.22, 0.18)
    return jnp.clip(array, -bound, bound).astype(held_as)


def setup_inputs(seed: int = 0) -> dict:
    key_of = jax.random.split(jax.random.key(seed), 17)
    return {
        "hidden": normal_values(key_of[0], (PAIRS, MODS, SLOTS, D), 1.0, 6.0, ((0, 64), (1, 2))),
        "text_counts": draw_text_counts(jax.random.fold_in(key_of[16], 71), 0),
        "region_counts": draw_region_counts(jax.random.fold_in(key_of[16], 71), 0),
        "qkv_weight": normal_values(key_of[3], (LAYERS, D, 3 * D), D ** -0.5, 0.21875),
        "qv_bias": normal_values(key_of[4], (LAYERS, 2 * D), 0.5, 3.0),
        "out_weight": normal_values(key_of[5], (LAYERS, D, D), (max(D // 64, 1)) ** -0.5, 1.75),
        "out_bias": normal_values(key_of[6], (LAYERS, D), 0.3, 2.0),
        "norm1_gain": jnp.clip(1.0 + 0.1 * jax.random.normal(key_of[7], (LAYERS, D), jnp.float32), 0.5, 1.5).astype(jnp.bfloat16),
        "norm1_bias": normal_values(key_of[8], (LAYERS, D), 0.3, 2.0),
        "up_weight": normal_values(key_of[9], (LAYERS, D, FF), D ** -0.5, 0.21875),
        "up_bias": normal_values(key_of[10], (LAYERS, FF), 0.5, 3.0),
        "down_weight": normal_values(key_of[11], (LAYERS, FF, D), FF ** -0.5, 0.109375),
        "down_bias": normal_values(key_of[12], (LAYERS, D), 0.3, 2.0),
        "norm2_gain": jnp.clip(1.0 + 0.1 * jax.random.normal(key_of[13], (LAYERS, D), jnp.float32), 0.5, 1.5).astype(jnp.bfloat16),
        "norm2_bias": normal_values(key_of[14], (LAYERS, D), 0.3, 2.0),
        "out_grad": normal_values(key_of[15], (PAIRS, MODS, SLOTS, D), 1.0, 6.0, ((0, 64), (1, 2))),
    }


norm_epsilon = 1e-06
masked_value = -1000000000.0

@jax.custom_vjp
def low(v):
    return lax.optimization_barrier(v.astype(jnp.bfloat16)).astype(jnp.float32)

@jax.custom_vjp
def low_back(v):
    return v

def low_keep(v):
    return (low(v), None)

def low_pass(kept, grad):
    return (grad,)

def back_keep(v):
    return (v, None)

def back_low(kept, grad):
    return (low(grad),)
low.defvjp(low_keep, low_pass)
low_back.defvjp(back_keep, back_low)

def layer_norm(values, scaling, offset):
    centre = values - lax.optimization_barrier(jnp.mean(values, -1, keepdims=True))
    spread = lax.optimization_barrier(jnp.mean(centre * centre, -1, keepdims=True))
    return centre * lax.rsqrt(spread + norm_epsilon) * scaling + offset

def attend_pair(inputs):
    query_rows, key_rows, value_rows, key_mask = inputs
    raw_scores = jnp.einsum('qhe,khe->hqk', query_rows, key_rows, precision=lax.Precision.HIGHEST) * HEAD_DIM ** (-0.5)
    scores = low_back(raw_scores)
    scores = jnp.where(key_mask[None, None, :] > 0.5, scores, masked_value)
    highest = lax.optimization_barrier(jnp.max(scores, -1, keepdims=True))
    exponent = jnp.exp(scores - highest)
    weights = low(exponent / lax.optimization_barrier(jnp.sum(exponent, -1, keepdims=True)))
    return jnp.einsum('hqk,khe->qhe', weights, value_rows, precision=lax.Precision.HIGHEST)

def forward(live_mask, hidden_rows, qkv_weight, qv_bias, out_weight, out_bias, norm1_gain, norm1_bias, up_weight, up_bias, down_weight, down_bias, norm2_gain, norm2_bias):
    pair_count = hidden_rows.shape[0]
    slot_count = hidden_rows.shape[2]
    key_mask = live_mask.reshape(pair_count, 2 * slot_count)
    row_mask = live_mask.reshape(-1, 1)
    current = hidden_rows.reshape(-1, D)
    for depth in range(LAYERS):
        zero_part = jnp.zeros((D,), jnp.float32)
        merged_bias = jnp.concatenate([qv_bias[depth, :D], zero_part, qv_bias[depth, D:]])
        merged = low(low_back(jnp.dot(current, qkv_weight[depth], precision=lax.Precision.HIGHEST) + merged_bias))
        split_heads = merged.reshape(pair_count, 2 * slot_count, 3, HEADS, HEAD_DIM)
        context = lax.map(jax.checkpoint(attend_pair), (split_heads[:, :, 0], split_heads[:, :, 1], split_heads[:, :, 2], key_mask))
        context = low(low_back(context.reshape(-1, D)))
        attention = low_back(jnp.dot(context, out_weight[depth], precision=lax.Precision.HIGHEST) + out_bias[depth])
        first_norm = layer_norm(current + attention, norm1_gain[depth], norm1_bias[depth])
        pre_gelu = low_back(jnp.dot(low(first_norm), up_weight[depth], precision=lax.Precision.HIGHEST) + up_bias[depth])
        activated = low(jax.nn.gelu(pre_gelu, approximate=False))
        branch = low_back(jnp.dot(activated, down_weight[depth], precision=lax.Precision.HIGHEST) + down_bias[depth])
        current = layer_norm(first_norm + branch, norm2_gain[depth], norm2_bias[depth]) * row_mask
        if depth + 1 < LAYERS:
            current = low(current)
    return current.reshape(hidden_rows.shape)

def reference(hidden, text_counts, region_counts, qkv_weight, qv_bias, out_weight, out_bias, norm1_gain, norm1_bias, up_weight, up_bias, down_weight, down_bias, norm2_gain, norm2_bias, out_grad):
    slot_index = jnp.arange(SLOTS, dtype=jnp.int32)
    counts = jnp.stack([text_counts, region_counts], 1).astype(jnp.int32)
    live_mask = (slot_index[None, None, :] < counts[:, :, None]).astype(jnp.float32)
    primals = (hidden, qkv_weight, qv_bias, out_weight, out_bias, norm1_gain, norm1_bias, up_weight, up_bias, down_weight, down_bias, norm2_gain, norm2_bias)
    primals = tuple((element.astype(jnp.float32) for element in primals))
    result, pullback = jax.vjp(partial(forward, live_mask), *primals)
    gradients = pullback(out_grad.astype(jnp.float32))
    return (result.astype(jnp.bfloat16), gradients[0].astype(jnp.bfloat16), gradients[1], gradients[2], gradients[3], gradients[4], gradients[5], gradients[6], gradients[7], gradients[8], gradients[9], gradients[10], gradients[11], gradients[12])
```

```python
import functools
from functools import partial

import jax
import jax.numpy as jnp
from jax import lax
from jax.experimental import pallas as pl
from jax.experimental.pallas import tpu as pltpu
from jax.sharding import PartitionSpec as P

MESH = pl.DeviceIdType.MESH
LANES = 128

def place():
    mod, batch = lax.axis_index("mod"), lax.axis_index("batch")
    return mod * 2 + lax.rem(batch // 2, 2), batch // 16, lax.rem(batch // 4, 4), lax.rem(batch, 2)

def device(x, y, z, core):
    return (x // 2, y * 16 + z * 4 + lax.rem(x, 2) * 2 + core)

def near(v):
    return v + 1 - 2 * lax.rem(v, 2)

def neighbours():
    x, y, z, core = place()
    targets = [device(near(x), y, z, core), device(x, near(y), z, core), device(x, y, near(z), core),
               device(3 - x, y, z, core), device(x, 3 - y, z, core), device(x, y, 3 - z, core)]
    bits = [lax.rem((v + 1) // 2, 2) for v in (x, y, z)] + [v // 2 for v in (x, y, z)]
    return targets, bits, device(x, y, z, 1 - core), core

class Stream:
    def __init__(self, blocks, rows):
        self.blocks, self.rows = blocks, rows
        self.half = blocks // 2
        self.part = self.half // 6
        assert self.part % 2 == 0
        self.shapes = []
        r, b = rows, self.part
        for s in range(4):
            r //= 2
            self.shapes.append((b, r))
        b //= 2
        self.shapes.append((b, r))
        self.shapes.append((b, r))

    def scratch(self):
        return [pltpu.VMEM((self.half, self.rows, LANES), jnp.bfloat16),
                pltpu.VMEM((self.half, self.rows, LANES), jnp.bfloat16)] + [
                pltpu.VMEM((6, b, r, LANES), jnp.bfloat16) for b, r in self.shapes] + [
                pltpu.SemaphoreType.DMA((6, 8)), pltpu.SemaphoreType.DMA((6, 8)),
                pltpu.SemaphoreType.DMA((6, 6)), pltpu.SemaphoreType.DMA((6, 6))]

def ar_kernel(stream, g_ref, o_ref, acc, corebuf, r0, r1, r2, r3, r4, r5, ssem, rsem, sag, rag):
    S = stream
    recv = [r0, r1, r2, r3, r4, r5]
    targets, bits, sibling, core = neighbours()
    bar = pltpu.get_barrier_semaphore()
    for t in targets + [sibling]:
        pl.semaphore_signal(bar, inc=1, device_id=t, device_id_type=MESH)
    pl.semaphore_wait(bar, 7)
    width = S.part
    def remote(src, dst, a, b, t):
        return pltpu.make_async_remote_copy(src, dst, a, b, device_id=t, device_id_type=MESH)
    cc, lc = [], []
    for p in range(6):
        c = remote(g_ref.at[pl.ds((1 - core) * S.half + p * width, width)], corebuf.at[pl.ds(p * width, width)], ssem.at[p, 0], rsem.at[p, 0], sibling)
        c.start(); cc.append(c)
        l = pltpu.make_async_copy(g_ref.at[pl.ds(core * S.half + p * width, width)], acc.at[pl.ds(p * width, width)], ssem.at[p, 7])
        l.start(); lc.append(l)
    reg = [[p * width, 0] for p in range(6)]
    cur = (width, S.rows)
    def add(dst, src, b, rows, chunk=48):
        n = rows // chunk
        def body(i, _):
            k, r = i // n, lax.rem(i, n) * chunk
            dst(k, r, chunk)[...] = dst(k, r, chunk)[...] + src(k, r, chunk)[...]
            return 0
        lax.fori_loop(0, b * n, body, 0)
    pending = {}
    def begin(p, s):
        b, r = S.shapes[s]
        d = (p + s) % 6
        bit = bits[d]
        bo, ro = reg[p]
        if s < 4:
            src = acc.at[pl.ds(bo, b), pl.ds(pl.multiple_of(ro + (1 - bit) * r, 16), r)]
            reg[p] = [bo, ro + bit * r]
        elif s == 4:
            src = acc.at[pl.ds(bo + (1 - bit) * b, b), pl.ds(pl.multiple_of(ro, 16), r)]
            reg[p] = [bo + bit * b, ro]
        else:
            src = acc.at[pl.ds(bo, b), pl.ds(pl.multiple_of(ro, 16), r)]
        c = remote(src, recv[s].at[p], ssem.at[p, s + 1], rsem.at[p, s + 1], targets[d])
        c.start()
        pending[p, s] = c
    def finish(p, s):
        b, r = S.shapes[s]
        bo, ro = reg[p]
        c = pending.pop((p, s))
        if s == 5: c.wait()
        else:
            c.wait_recv()
            c.wait_send()
        ch = 48
        add(lambda k, rr, n: acc.at[bo + k, pl.ds(pl.multiple_of(ro + rr, 16), n)], lambda k, rr, n: recv[s].at[p, k, pl.ds(pl.multiple_of(rr, 16), n)], b, r, ch)
    for p in range(6):
        cc[p].wait(); lc[p].wait()
        add(lambda k, rr, n: acc.at[p * width + k, pl.ds(pl.multiple_of(rr, 16), n)], lambda k, rr, n: corebuf.at[p * width + k, pl.ds(pl.multiple_of(rr, 16), n)], width, S.rows, 192)
        begin(p, 0)
    for s in range(6):
        for p in range(6):
            finish(p, s)
            if s < 5: begin(p, s + 1)
            else:
                b, r = S.shapes[5]
                bo, ro = reg[p]
                l = pltpu.make_async_copy(acc.at[pl.ds(bo, b), pl.ds(pl.multiple_of(ro, 16), r)],
                                          o_ref.at[pl.ds(core * S.half + bo, b), pl.ds(pl.multiple_of(ro, 16), r)], sag.at[p, 5])
                l.start(); pending[p, "l"] = l
    def gather(p, s):
        b, r = S.shapes[s]
        bo, ro = reg[p]
        d = (p + s) % 6
        ref = o_ref.at[pl.ds(core * S.half + bo, b), pl.ds(pl.multiple_of(ro, 16), r)]
        c = remote(ref, ref, sag.at[p, s], rag.at[p, s], targets[d])
        c.start(); pending[p, s] = c
        bit = bits[d]
        if s == 4: reg[p] = [bo - bit * b, ro]
        else: reg[p] = [bo, ro - bit * r]
    for p in range(6):
        pending.pop((p, "l")).wait()
        gather(p, 4)
    for s in range(4, -1, -1):
        for p in range(6):
            pending.pop((p, s)).wait()
            if s > 0: gather(p, s - 1)
            else:
                ref = o_ref.at[pl.ds(core * S.half + p * width, width)]
                c = remote(ref, ref, ssem.at[p, 7], rag.at[p, 5], sibling)
                c.start(); pending[p, "c"] = c
    for p in range(6):
        pending.pop((p, "c")).wait()

def all_reduce(g, cid=1):
    S = Stream(g.shape[0], g.shape[1])
    return pl.pallas_call(functools.partial(ar_kernel, S), out_shape=jax.ShapeDtypeStruct(g.shape, g.dtype),
        in_specs=[pl.BlockSpec(memory_space=pl.ANY)], out_specs=pl.BlockSpec(memory_space=pl.ANY),
        scratch_shapes=S.scratch(),
        compiler_params=pltpu.CompilerParams(collective_id=cid, has_side_effects=True, vmem_limit_bytes=60*2**20))(g)


HEADS = 12
HEAD_DIM = 64


norm_epsilon = 1e-06
masked_value = -1000000000.0


def partner(x, axis, distance):
    return lax.ppermute(x, axis, [(i, i ^ 1 << distance) for i in range(lax.axis_size(axis))])


def layer_norm(values, scaling, offset):
    centre = values - jnp.mean(values, -1, keepdims=True)
    spread = jnp.mean(centre * centre, -1, keepdims=True)
    return centre * lax.rsqrt(spread + norm_epsilon) * scaling + offset


def column_product(left, right):
    return lax.dot_general(
        left, right, (((0,), (0,)), ((), ())), preferred_element_type=jnp.float32
    )


def row_product(left, right):
    return lax.dot_general(
        left, right, (((1,), (1,)), ((), ())), preferred_element_type=jnp.float32
    )


def pair_scores(queries, key_rows, key_mask):
    raw_scores = jnp.einsum(
        "pqhe,pkhe->phqk", queries, key_rows, preferred_element_type=jnp.float32
    ) * HEAD_DIM ** (-0.5)
    return jnp.where(key_mask[:, None, None, :] > 0.5, raw_scores, masked_value)


def body(
    hidden,
    text_counts,
    region_counts,
    qkv_weight,
    qv_bias,
    out_weight,
    out_bias,
    norm1_gain,
    norm1_bias,
    up_weight,
    up_bias,
    down_weight,
    down_bias,
    norm2_gain,
    norm2_bias,
    out_grad,
):
    pair_count = hidden.shape[0]
    slot_count = hidden.shape[2]
    model_width = hidden.shape[3]
    depth_count = qkv_weight.shape[0]
    row_count = pair_count * slot_count
    head_shape = (pair_count, slot_count, HEADS, HEAD_DIM)
    score_scale = HEAD_DIM ** (-0.5)
    modality = lax.axis_index("mod")
    own_counts = jnp.where(modality == 0, text_counts, region_counts)
    other_counts = jnp.where(modality == 0, region_counts, text_counts)
    slot_index = jnp.arange(slot_count, dtype=jnp.int32)
    own_live = (slot_index[None, :] < own_counts[:, None]).astype(jnp.float32)
    other_live = (slot_index[None, :] < other_counts[:, None]).astype(jnp.float32)
    key_mask = jnp.concatenate([own_live, other_live], 1)
    row_mask = own_live.reshape(row_count, 1)
    current = hidden.reshape(row_count, model_width)
    depth = 0
    merged_bias = jnp.concatenate(
        [
            qv_bias[depth, :model_width].astype(jnp.float32),
            jnp.zeros((model_width,), jnp.float32),
            qv_bias[depth, model_width:].astype(jnp.float32),
        ]
    )
    merged = (
        jnp.dot(current, qkv_weight[depth], preferred_element_type=jnp.float32) + merged_bias
    ).astype(jnp.bfloat16)
    queries = merged[:, :model_width].reshape(head_shape)
    own_keys = merged[:, model_width : 2 * model_width]
    own_values = merged[:, 2 * model_width :]
    partner_keys, partner_values = partner((own_keys, own_values), "mod", 0)
    key_rows = jnp.concatenate([own_keys.reshape(head_shape), partner_keys.reshape(head_shape)], 1)
    value_rows = jnp.concatenate(
        [own_values.reshape(head_shape), partner_values.reshape(head_shape)], 1
    )
    scores = pair_scores(queries, key_rows, key_mask)
    highest = jnp.max(scores, -1, keepdims=True)
    log_total = highest + jnp.log(jnp.sum(jnp.exp(scores - highest), -1, keepdims=True))
    weights_low = jnp.exp(scores - log_total).astype(jnp.bfloat16)
    context = jnp.einsum(
        "phqk,pkhe->pqhe", weights_low, value_rows, preferred_element_type=jnp.float32
    )
    context = context.reshape(row_count, model_width).astype(jnp.bfloat16)
    attention = jnp.dot(context, out_weight[depth], preferred_element_type=jnp.float32) + out_bias[
        depth
    ].astype(jnp.float32)
    first_sum = current.astype(jnp.float32) + attention
    first_norm = layer_norm(
        first_sum, norm1_gain[depth].astype(jnp.float32), norm1_bias[depth].astype(jnp.float32)
    )
    first_low = first_norm.astype(jnp.bfloat16)
    pre_gelu = jnp.dot(first_low, up_weight[depth], preferred_element_type=jnp.float32) + up_bias[
        depth
    ].astype(jnp.float32)
    activated = jax.nn.gelu(pre_gelu, approximate=False).astype(jnp.bfloat16)
    second_sum = (
        first_norm
        + jnp.dot(activated, down_weight[depth], preferred_element_type=jnp.float32)
        + down_bias[depth].astype(jnp.float32)
    )
    layer_result = (
        layer_norm(
            second_sum, norm2_gain[depth].astype(jnp.float32), norm2_bias[depth].astype(jnp.float32)
        )
        * row_mask
    )
    kept_pair = None
    saved = [
        (
            current,
            merged,
            kept_pair,
            log_total,
            context,
            first_sum,
            first_low,
            pre_gelu,
            activated,
            second_sum,
        )
    ]
    current = layer_result.astype(jnp.bfloat16)
    layer_out = current.reshape(hidden.shape)
    upstream = out_grad.reshape(row_count, model_width).astype(jnp.float32)
    per_depth = [None] * depth_count
    for depth in reversed(range(depth_count)):
        (
            layer_input,
            merged,
            kept_pair,
            log_total,
            context,
            first_sum,
            first_low,
            pre_gelu,
            activated,
            second_sum,
        ) = saved[depth]
        masked_grad = upstream * row_mask
        second_value, second_pull = jax.vjp(
            layer_norm,
            second_sum,
            norm2_gain[depth].astype(jnp.float32),
            norm2_bias[depth].astype(jnp.float32),
        )
        second_grad, gain2_grad, bias2_grad = second_pull(masked_grad)
        branch_low = second_grad.astype(jnp.bfloat16)
        down_grad = column_product(activated, branch_low)
        down_bias_grad = jnp.sum(branch_low.astype(jnp.float32), 0)
        gelu_value, gelu_pull = jax.vjp(partial(jax.nn.gelu, approximate=False), pre_gelu)
        pre_grad = gelu_pull(row_product(branch_low, down_weight[depth]))[0].astype(jnp.bfloat16)
        up_grad = column_product(first_low, pre_grad)
        up_bias_grad = jnp.sum(pre_grad.astype(jnp.float32), 0)
        norm_grad = row_product(pre_grad, up_weight[depth]) + second_grad
        ffn_part = (up_grad, up_bias_grad, down_grad, down_bias_grad, gain2_grad, bias2_grad)
        first_value, first_pull = jax.vjp(
            layer_norm,
            first_sum,
            norm1_gain[depth].astype(jnp.float32),
            norm1_bias[depth].astype(jnp.float32),
        )
        sum_grad, gain1_grad, bias1_grad = first_pull(norm_grad)
        attention_low = sum_grad.astype(jnp.bfloat16)
        out_weight_grad = column_product(context, attention_low)
        out_bias_grad = jnp.sum(attention_low.astype(jnp.float32), 0)
        context_grad = (
            row_product(attention_low, out_weight[depth]).astype(jnp.bfloat16).reshape(head_shape)
        )
        queries = merged[:, :model_width].reshape(head_shape)
        own_keys = merged[:, model_width : 2 * model_width]
        own_values = merged[:, 2 * model_width :]
        partner_keys, partner_values = partner((own_keys, own_values), "mod", 0)
        key_rows = jnp.concatenate(
            [own_keys.reshape(head_shape), partner_keys.reshape(head_shape)], 1
        )
        value_rows = jnp.concatenate(
            [own_values.reshape(head_shape), partner_values.reshape(head_shape)], 1
        )
        scores = pair_scores(queries, key_rows, key_mask)
        weights_full = jnp.exp(scores - log_total)
        weights_low = weights_full.astype(jnp.bfloat16)
        weight_grad = jnp.einsum(
            "pqhe,pkhe->phqk", context_grad, value_rows, preferred_element_type=jnp.float32
        )
        value_grad = jnp.einsum(
            "phqk,pqhe->pkhe", weights_low, context_grad, preferred_element_type=jnp.float32
        )
        score_grad = weights_full * (
            weight_grad - jnp.sum(weights_full * weight_grad, -1, keepdims=True)
        )
        score_grad = score_grad.astype(jnp.bfloat16)
        query_grad = (
            jnp.einsum("phqk,pkhe->pqhe", score_grad, key_rows, preferred_element_type=jnp.float32)
            * score_scale
        )
        key_grad = (
            jnp.einsum("phqk,pqhe->pkhe", score_grad, queries, preferred_element_type=jnp.float32)
            * score_scale
        )
        back_keys, back_values = (
            partner(key_grad[:, slot_count:].astype(jnp.bfloat16), "mod", 0).astype(jnp.float32),
            partner(value_grad[:, slot_count:].astype(jnp.bfloat16), "mod", 0).astype(jnp.float32),
        )
        own_key_grad = (key_grad[:, :slot_count] + back_keys).reshape(row_count, model_width)
        own_value_grad = (value_grad[:, :slot_count] + back_values).reshape(row_count, model_width)
        merged_grad = jnp.concatenate(
            [query_grad.reshape(row_count, model_width), own_key_grad, own_value_grad], 1
        ).astype(jnp.bfloat16)
        merged_weight_grad = column_product(layer_input, merged_grad)
        merged_column = jnp.sum(merged_grad.astype(jnp.float32), 0)
        merged_bias_grad = jnp.concatenate(
            [merged_column[:model_width], merged_column[2 * model_width :]]
        )
        attention_part = (
            merged_weight_grad,
            merged_bias_grad,
            out_weight_grad,
            out_bias_grad,
            gain1_grad,
            bias1_grad,
        )
        per_depth[depth] = tuple(attention_part) + tuple(ffn_part)
        upstream = row_product(merged_grad, qkv_weight[depth]) + sum_grad
    input_grad = upstream.astype(jnp.bfloat16).reshape(hidden.shape)
    stacked = [jnp.stack([per_depth[0][member]]) for member in range(12)]
    def blocks(matrix):
        rows, columns = matrix.shape
        cut = matrix.astype(jnp.bfloat16).reshape(rows // 768, 768, columns // LANES, LANES)
        return cut.transpose(0, 2, 1, 3).reshape(-1, 768, LANES)

    def unblock(cut, rows, columns):
        cut = cut.reshape(rows // 768, columns // LANES, 768, LANES).transpose(0, 2, 1, 3)
        return cut.reshape(1, rows, columns).astype(jnp.float32)

    small = [1, 3, 4, 5, 7, 9, 10, 11]
    summed = lax.psum(tuple(stacked[i] for i in small), ("mod", "batch"))
    for i, value in zip(small, summed):
        stacked[i] = value
    shapes = {0: (768, 2304), 2: (768, 768), 6: (768, 3072), 8: (3072, 768)}
    packed = jnp.concatenate([blocks(stacked[i][0]) for i in shapes], 0)
    packed = all_reduce(packed)
    start = 0
    for i, (rows, columns) in shapes.items():
        count = rows * columns // (768 * LANES)
        stacked[i] = unblock(packed[start : start + count], rows, columns)
        start += count
    return (
        layer_out,
        input_grad,
        stacked[0],
        stacked[1],
        stacked[2],
        stacked[3],
        stacked[4],
        stacked[5],
        stacked[6],
        stacked[7],
        stacked[8],
        stacked[9],
        stacked[10],
        stacked[11],
    )


def solution(mesh):
    return jax.shard_map(
        body,
        mesh=mesh,
        in_specs=(
            P("batch", "mod", None, None),
            P("batch"),
            P("batch"),
            P(),
            P(),
            P(),
            P(),
            P(),
            P(),
            P(),
            P(),
            P(),
            P(),
            P(),
            P(),
            P("batch", "mod", None, None),
        ),
        out_specs=(
            P("batch", "mod", None, None),
            P("batch", "mod", None, None),
            P(),
            P(),
            P(),
            P(),
            P(),
            P(),
            P(),
            P(),
            P(),
            P(),
            P(),
            P(),
        ),
        check_vma=False,
    )
```

```python
import functools
import math

import jax
import jax.numpy as jnp
from jax import lax
from jax.experimental import pallas as pl
from jax.experimental.pallas import tpu as pltpu
from jax.sharding import PartitionSpec as P

MESH = pl.DeviceIdType.MESH

BF, F32 = jnp.bfloat16, jnp.float32
LANES = 128
D, HEADS, FF, SLOTS = 768, 12, 3072, 128
WHOLE = 3
QROWS = WHOLE * 256 + 128
KROWS = QROWS + 128
EPS = 1e-6
MASKED = -1e9
LOG2E = math.log2(math.e)
SCALE = 0.125
UF, UB, GT, LR, LU = 6, 3, 768, 128, 1

def nn(a, b):
    return lax.dot_general(a, b, (((1,), (0,)), ((), ())), preferred_element_type=F32)
def nt(a, b):
    return lax.dot_general(a, b, (((1,), (1,)), ((), ())), preferred_element_type=F32)
def tn(a, b):
    return lax.dot_general(a, b, (((0,), (0,)), ((), ())), preferred_element_type=F32)

def gelu_pair(v):
    a = jnp.abs(v)
    e = jnp.exp2(v * v * (-0.5 * LOG2E))
    d = 1.0 + (0.3275911 / math.sqrt(2.0)) * a
    t = pl.reciprocal(d, approx=True)
    t = t * (2.0 - d * t)
    poly = ((((0.5 * 1.061405429 * t + 0.5 * -1.453152027) * t + 0.5 * 1.421413741) * t + 0.5 * -0.284496736) * t + 0.5 * 0.254829592) * t
    tail = poly * e
    cdf = jnp.where(v >= 0, 1.0 - tail, tail)
    return v * cdf, cdf + v * e * (1.0 / math.sqrt(2.0 * math.pi))

VEC = dict(q=0, v=768, out=1536, g1=2304, b1=3072, up=3840, down=6912, g2=7680, b2=8448)
VLEN = 9216

def normalize(s):
    centre = s - jnp.mean(s, -1, keepdims=True)
    r = lax.rsqrt(jnp.mean(centre * centre, -1, keepdims=True) + EPS)
    return centre * r, r

def norm_back(g, n, r):
    return r * (g - jnp.mean(g, -1, keepdims=True) - n * jnp.mean(g * n, -1, keepdims=True))

def compute_kernel(stop, hid, rhid, og, rog, tc, rc, wqkv_h, qvb, wo_h, bo_l, g1_l, b1_l, wup_h, bup_l, wdn_h, bdn_l, g2_l, b2_l,
                   y_ref, yo_ref, ig_ref, igo_ref, mid_ref, grad_ref, vec,
                   x, xt, merged, ctx, fsum, flow, flowt, act, pre, branch, dsec, mid32,
                   wqkv, wo, wup, wdn, ogv, stage, bqkv, bup, small, colsum, wsem, iosem, gsem):
    mod = lax.axis_index("mod")
    bqkv[:, 0:768] = qvb[:, 0:768].astype(F32)
    bqkv[:, 768:1536] = jnp.zeros((1, 768), F32)
    bqkv[:, 1536:2304] = qvb[:, 768:1536].astype(F32)
    bup[...] = bup_l[...].astype(F32)
    for k, l in enumerate((bo_l, g1_l, b1_l, bdn_l, g2_l, b2_l)):
        small[k] = l[...].astype(F32)
    bo, g1, b1, bdn, g2, b2 = (small.at[k] for k in range(6))
    def pair_of(i):
        return i + mod * (6 - 2 * i)
    def recv_of(i, n):
        return i + mod * (n - 1 - 2 * i)
    loads = []
    for k, (src, dst) in enumerate([(wqkv_h, wqkv), (wo_h, wo), (wup_h, wup), (wdn_h, wdn)]):
        loads.append(pltpu.make_async_copy(src, dst, wsem.at[k]))
    xin = []
    for i in range(4):
        xin.append(pltpu.make_async_copy(hid.at[pair_of(i)], x.at[pl.ds(i * 256, 128)], iosem.at[i]))
        xin.append(pltpu.make_async_copy(rhid.at[recv_of(i, 4)], x.at[pl.ds(i * 256 + 128, 128)], iosem.at[4 + i]))
    ogin = []
    for i in range(4):
        ogin.append(pltpu.make_async_copy(og.at[pair_of(i)], ogv.at[pl.ds(i * 256, 128)], iosem.at[8 + i]))
        if i < 3:
            ogin.append(pltpu.make_async_copy(rog.at[recv_of(i, 3)], ogv.at[pl.ds(i * 256 + 128, 128)], iosem.at[12 + i]))
    for c in xin: c.start()
    loads[0].start()
    for c in loads[1:]: c.start()
    for c in ogin: c.start()
    for c in xin: c.wait()
    loads[0].wait()

    def own_count(i):
        return jnp.where(mod == 0, tc[pair_of(i)], rc[pair_of(i)])
    def other_count(i):
        return jnp.where(mod == 0, rc[pair_of(i)], tc[pair_of(i)])

    def p1(j, _):
        cols = pl.ds(pl.multiple_of(j * 768, 768), 768)
        merged[:, cols] = (nn(x[...], wqkv[:, cols]) + bqkv[:, cols]).astype(BF)
        return 0
    lax.fori_loop(0, 3, p1, 0)
    if stop <= 1:
        for c in loads[1:] + ogin: c.wait()
        return
    lane = lax.broadcasted_iota(jnp.int32, (256, 128), 1)
    row = lax.broadcasted_iota(jnp.int32, (256, 256), 0)
    def key_live(i, nq):
        r = lax.broadcasted_iota(jnp.int32, (256, nq), 0)
        return r < jnp.where(r < 128, own_count(i), 128 + other_count(i))
    zero = jnp.zeros((), BF)
    def half(v, h):
        l = lax.broadcasted_iota(jnp.int32, v.shape, 1)
        return jnp.where((l < 64) if h == 0 else (l >= 64), v, zero)
    def attend(i, hp, nq):
        base = pl.multiple_of(i * 256, 256)
        c0 = pl.multiple_of(hp * 128, 128)
        q = merged[pl.ds(base, nq), pl.ds(c0, 128)]
        k = merged[pl.ds(base, 256), pl.ds(c0 + 768, 128)]
        v = merged[pl.ds(base, 256), pl.ds(c0 + 1536, 128)]
        live = key_live(i, nq)
        out = None
        for h in range(2):
            s = nt(half(k, h), q) * (SCALE * LOG2E)
            s = jnp.where(live, s, MASKED)
            m = jnp.max(s, 0, keepdims=True)
            e = jnp.exp2(s - m)
            p = (e * (1.0 / jnp.sum(e, 0, keepdims=True))).astype(BF)
            o = tn(p, half(v, h))
            out = o if out is None else out + o
        ctx[pl.ds(base, nq), pl.ds(c0, 128)] = out.astype(BF)
    def p2(t, _):
        for u in range(UF): attend(t // (6 // UF), lax.rem(t, 6 // UF) * UF + u, 256)
        return 0
    lax.fori_loop(0, WHOLE * 6 // UF, p2, 0)
    def p2m(t, _):
        for u in range(UF): attend(WHOLE, t * UF + u, 128)
        return 0
    lax.fori_loop(0, 6 // UF, p2m, 0)
    if stop <= 2:
        for c in loads[1:] + ogin: c.wait()
        return
    loads[1].wait()
    fsum[...] = x[0:QROWS, :].astype(F32) + nn(ctx[...], wo[...]) + bo[...]
    def p3(r, _):
        rows = pl.ds(pl.multiple_of(r * LR, LR), LR)
        n, _r = normalize(fsum[rows, :])
        flow[rows, :] = (n * g1[...] + b1[...]).astype(BF)
        return 0
    lax.fori_loop(0, QROWS // LR, p3, 0, unroll=LU)
    if stop <= 3:
        for c in loads[2:] + ogin: c.wait()
        return
    loads[2].wait()
    def p4(j, _):
        cols = pl.ds(pl.multiple_of(j * GT, GT), GT)
        a, d = gelu_pair(nn(flow[...], wup[:, cols]) + bup[:, cols])
        act[:, cols] = a.astype(BF)
        pre[:, cols] = d.astype(BF)
        return 0
    lax.fori_loop(0, FF // GT, p4, 0)
    if stop <= 4:
        for c in loads[3:] + ogin: c.wait()
        return
    loads[3].wait()
    for c in ogin: c.wait()
    dsec[...] = nn(act[...], wdn[...]) + bdn[...]
    colsum[...] = jnp.zeros_like(colsum)
    def fold(v):
        return v.reshape(v.shape[0] // 8, 8, v.shape[1]).sum(0)
    def p5(r, _):
        rows = pl.ds(pl.multiple_of(r * LR, LR), LR)
        slot = r * LR // 128
        i = slot // 2
        live = lax.broadcasted_iota(jnp.int32, (LR, 1), 0) + lax.rem(r * LR, 128) < jnp.where(lax.rem(slot, 2) == 0, own_count(i), other_count(i))
        livef = live.astype(F32)
        n, rr = normalize(fsum[rows, :])
        n, rr = normalize(n * g1[...] + b1[...] + dsec[rows, :])
        dout = ogv[rows, :].astype(F32) * livef
        ogv[rows, :] = ((n * g2[...] + b2[...]) * livef).astype(BF)
        colsum[0] += fold(dout * n)
        colsum[1] += fold(dout)
        ds = norm_back(dout * g2[...], n, rr)
        dsec[rows, :] = ds
        low = ds.astype(BF)
        branch[rows, :] = low
        colsum[2] += fold(low.astype(F32))
        return 0
    lax.fori_loop(0, QROWS // LR, p5, 0, unroll=LU)
    for k, name in enumerate(("g2", "b2", "down")):
        vec[:, VEC[name]:VEC[name] + 768] = jnp.sum(colsum[k], 0, keepdims=True)
    outs = []
    for i in range(4):
        outs.append(pltpu.make_async_copy(ogv.at[pl.ds(i * 256, 128)], y_ref.at[pair_of(i)], iosem.at[i]))
        if i < 3:
            outs.append(pltpu.make_async_copy(ogv.at[pl.ds(i * 256 + 128, 128)], yo_ref.at[i + mod * (2 - 2 * i)], iosem.at[4 + i]))
    for c in outs: c.start()
    for c in outs: c.wait()
    if stop <= 5: return
    def gcopy(slot, block):
        return pltpu.make_async_copy(stage.at[slot], grad_ref.at[pl.ds(block, 6)], gsem.at[slot])
    def put(t, block, value, first):
        slot = lax.rem(t, 2)
        @pl.when(jnp.logical_not(first))
        def _(): gcopy(slot, block).wait()
        for b in range(6): stage[slot, b] = value[:, b * 128:(b + 1) * 128]
        gcopy(slot, block).start()
    def p6(t, _):
        rows = pl.ds(pl.multiple_of(t * 768, 768), 768)
        put(t, 24 + t * 6, tn(act[:, rows], branch[...]).astype(BF), t < 2)
        return 0
    lax.fori_loop(0, 4, p6, 0)
    if stop <= 6:
        for s in range(2): gcopy(s, 0).wait()
        return
    flowt[...] = flow[...].T
    def p7(j, _):
        cols = pl.ds(pl.multiple_of(j * 768, 768), 768)
        pg = nt(branch[...], wdn[cols, :]) * pre[:, cols].astype(F32)
        low = pg.astype(BF)
        pre[:, cols] = low
        vec[:, pl.ds(pl.multiple_of(VEC["up"] + j * 768, 768), 768)] = jnp.sum(low.astype(F32), 0, keepdims=True)
        put(j, 6 * j, nn(flowt[...], low).astype(BF), False)
        return 0
    lax.fori_loop(0, 4, p7, 0)
    if stop <= 7:
        for s in range(2): gcopy(s, 0).wait()
        return
    dsec[...] += nt(pre[...], wup[...])
    colsum[...] = jnp.zeros_like(colsum)
    def p8(r, _):
        rows = pl.ds(pl.multiple_of(r * LR, LR), LR)
        g = dsec[rows, :]
        n, rr = normalize(fsum[rows, :])
        colsum[0] += fold(g * n)
        colsum[1] += fold(g)
        df = norm_back(g * g1[...], n, rr)
        dsec[rows, :] = df
        low = df.astype(BF)
        branch[rows, :] = low
        colsum[2] += fold(low.astype(F32))
        return 0
    lax.fori_loop(0, QROWS // LR, p8, 0, unroll=LU)
    for k, name in enumerate(("g1", "b1", "out")):
        vec[:, VEC[name]:VEC[name] + 768] = jnp.sum(colsum[k], 0, keepdims=True)
    flow[...] = nt(branch[...], wo[...]).astype(BF)
    if stop <= 8:
        for s in range(2): gcopy(s, 0).wait()
        return
    put(0, 48, tn(ctx[...], branch[...]).astype(BF), False)
    if stop <= 9:
        for s in range(2): gcopy(s, 0).wait()
        return
    def attend_back(i, hp, nq):
        base = pl.multiple_of(i * 256, 256)
        c0 = pl.multiple_of(hp * 128, 128)
        qs, ks, vs = (pl.ds(c0 + 768 * m, 128) for m in range(3))
        q = merged[pl.ds(base, nq), qs]
        k = merged[pl.ds(base, 256), ks]
        v = merged[pl.ds(base, 256), vs]
        dc = flow[pl.ds(base, nq), pl.ds(c0, 128)]
        live = key_live(i, nq)
        dq = dk = dv = None
        for h in range(2):
            kh = half(k, h)
            s = nt(kh, q) * (SCALE * LOG2E)
            s = jnp.where(live, s, MASKED)
            m = jnp.max(s, 0, keepdims=True)
            e = jnp.exp2(s - m)
            p = e * (1.0 / jnp.sum(e, 0, keepdims=True))
            dp = nt(half(v, h), dc)
            ds = (p * (dp - jnp.sum(p * dp, 0, keepdims=True))).astype(BF)
            a, b, c = nn(p.astype(BF), half(dc, h)), nn(ds, half(q, h)), tn(ds, kh)
            if h == 0: dv, dk, dq = a, b, c
            else: dv, dk, dq = dv + a, dk + b, dq + c
        merged[pl.ds(base, nq), qs] = (dq * SCALE).astype(BF)
        merged[pl.ds(base, 256), ks] = (dk * SCALE).astype(BF)
        merged[pl.ds(base, 256), vs] = dv.astype(BF)
        if nq < 256:
            merged[pl.ds(base + nq, 256 - nq), qs] = jnp.zeros((256 - nq, 128), BF)
    def p10(t, _):
        for u in range(UB): attend_back(t // (6 // UB), lax.rem(t, 6 // UB) * UB + u, 256)
        return 0
    lax.fori_loop(0, WHOLE * 6 // UB, p10, 0)
    def p10m(t, _):
        for u in range(UB): attend_back(WHOLE, t * UB + u, 128)
        return 0
    lax.fori_loop(0, 6 // UB, p10m, 0)
    if stop <= 10:
        for s in range(2): gcopy(s, 0).wait()
        return
    xt[...] = x[...].T
    def p11(j, _):
        cols = pl.ds(pl.multiple_of(j * 768, 768), 768)
        mg = merged[:, cols]
        put(j + 1, 54 + 6 * j, nn(xt[...], mg).astype(BF), False)
        @pl.when(j != 1)
        def _(): vec[:, pl.ds(pl.multiple_of((j // 2) * 768, 768), 768)] = jnp.sum(mg.astype(F32), 0, keepdims=True)
        return 0
    lax.fori_loop(0, 3, p11, 0)
    for s in range(2): gcopy(s, 0).wait()
    if stop <= 11: return
    g = nt(merged[...], wqkv[...])
    x[0:768, :] = (g[0:768] + dsec[0:768, :]).astype(BF)
    mid32[...] = g[768:896] + dsec[768:896, :]
    x[896:, :] = g[896:].astype(BF)
    outs = []
    for i in range(4):
        if i < 3: outs.append(pltpu.make_async_copy(x.at[pl.ds(i * 256, 128)], ig_ref.at[pair_of(i)], iosem.at[i]))
        outs.append(pltpu.make_async_copy(x.at[pl.ds(i * 256 + 128, 128)], igo_ref.at[recv_of(i, 4)], iosem.at[4 + i]))
    outs.append(pltpu.make_async_copy(mid32, mid_ref, iosem.at[8]))
    for c in outs: c.start()
    for c in outs: c.wait()

def compute(stop, hid, rhid, og, rog, tc, rc, wqkv, qvb, wo, bo, g1, b1, wup, bup, wdn, bdn, g2, b2):
    any_, vm, sm_ = (pl.BlockSpec(memory_space=m) for m in (pl.ANY, pltpu.VMEM, pltpu.SMEM))
    S = jax.ShapeDtypeStruct
    return pl.pallas_call(functools.partial(compute_kernel, stop),
        out_shape=(S((7, 128, 768), BF), S((3, 128, 768), BF), S((7, 128, 768), BF), S((4, 128, 768), BF), S((128, 768), F32),
                   S((72, 768, 128), BF), S((1, VLEN), F32)),
        in_specs=[any_] * 4 + [sm_] * 2 + [any_, vm, any_, vm, vm, vm, any_, vm, any_, vm, vm, vm],
        out_specs=(any_,) * 6 + (vm,),
        scratch_shapes=[pltpu.VMEM((KROWS, D), BF), pltpu.VMEM((D, KROWS), BF), pltpu.VMEM((KROWS, 3 * D), BF), pltpu.VMEM((QROWS, D), BF),
            pltpu.VMEM((QROWS, D), F32), pltpu.VMEM((QROWS, D), BF), pltpu.VMEM((D, QROWS), BF), pltpu.VMEM((QROWS, FF), BF), pltpu.VMEM((QROWS, FF), BF),
            pltpu.VMEM((QROWS, D), BF), pltpu.VMEM((QROWS, D), F32), pltpu.VMEM((128, D), F32),
            pltpu.VMEM((D, 3 * D), BF), pltpu.VMEM((D, D), BF), pltpu.VMEM((D, FF), BF), pltpu.VMEM((FF, D), BF), pltpu.VMEM((QROWS, D), BF),
            pltpu.VMEM((2, 6, 768, 128), BF), pltpu.VMEM((1, 3 * D), F32), pltpu.VMEM((1, FF), F32), pltpu.VMEM((6, 1, D), F32), pltpu.VMEM((3, 8, D), F32),
            pltpu.SemaphoreType.DMA((4,)), pltpu.SemaphoreType.DMA((16,)), pltpu.SemaphoreType.DMA((2,))],
        compiler_params=pltpu.CompilerParams(vmem_limit_bytes=62 * 2**20),
        )(hid, rhid, og, rog, tc, rc, wqkv, qvb, wo, bo, g1, b1, wup, bup, wdn, bdn, g2, b2)


def place():
    mod, batch = lax.axis_index("mod"), lax.axis_index("batch")
    return mod * 2 + lax.rem(batch // 2, 2), batch // 16, lax.rem(batch // 4, 4), lax.rem(batch, 2)

def device(x, y, z, core):
    return (x // 2, y * 16 + z * 4 + lax.rem(x, 2) * 2 + core)

def near(v):
    return v + 1 - 2 * lax.rem(v, 2)

def neighbours():
    x, y, z, core = place()
    targets = [device(near(x), y, z, core), device(x, near(y), z, core), device(x, y, near(z), core),
               device(3 - x, y, z, core), device(x, 3 - y, z, core), device(x, y, 3 - z, core)]
    bits = [lax.rem((v + 1) // 2, 2) for v in (x, y, z)] + [v // 2 for v in (x, y, z)]
    return targets, bits, device(x, y, z, 1 - core), core

class Stream:
    def __init__(self, blocks, rows):
        self.blocks, self.rows = blocks, rows
        self.half = blocks // 2
        self.part = self.half // 6
        assert self.part % 2 == 0
        self.shapes = []
        r, b = rows, self.part
        for s in range(4):
            r //= 2
            self.shapes.append((b, r))
        b //= 2
        self.shapes.append((b, r))
        self.shapes.append((b, r))

    def scratch(self):
        return [pltpu.VMEM((self.half, self.rows, LANES), jnp.bfloat16),
                pltpu.VMEM((self.half, self.rows, LANES), jnp.bfloat16)] + [
                pltpu.VMEM((6, b, r, LANES), jnp.bfloat16) for b, r in self.shapes] + [
                pltpu.SemaphoreType.DMA((6, 8)), pltpu.SemaphoreType.DMA((6, 8)),
                pltpu.SemaphoreType.DMA((6, 6)), pltpu.SemaphoreType.DMA((6, 6))]

def ar_kernel(stream, g_ref, v_ref, o_ref, vo_ref, vbuf, vss, vrs, acc, corebuf, r0, r1, r2, r3, r4, r5, ssem, rsem, sag, rag):
    S = stream
    recv = [r0, r1, r2, r3, r4, r5]
    targets, bits, sibling, core = neighbours()
    bar = pltpu.get_barrier_semaphore()
    for t in targets + [sibling]:
        pl.semaphore_signal(bar, inc=1, device_id=t, device_id_type=MESH)
    pl.semaphore_wait(bar, 7)
    width = S.part
    def remote(src, dst, a, b, t):
        return pltpu.make_async_remote_copy(src, dst, a, b, device_id=t, device_id_type=MESH)
    cc, lc = [], []
    for p in range(6):
        c = remote(g_ref.at[pl.ds((1 - core) * S.half + p * width, width)], corebuf.at[pl.ds(p * width, width)], ssem.at[p, 0], rsem.at[p, 0], sibling)
        c.start(); cc.append(c)
        l = pltpu.make_async_copy(g_ref.at[pl.ds(core * S.half + p * width, width)], acc.at[pl.ds(p * width, width)], ssem.at[p, 7])
        l.start(); lc.append(l)
    reg = [[p * width, 0] for p in range(6)]
    cur = (width, S.rows)
    def add(dst, src, b, rows, chunk=48):
        n = rows // chunk
        def body(i, _):
            k, r = i // n, lax.rem(i, n) * chunk
            dst(k, r, chunk)[...] = dst(k, r, chunk)[...] + src(k, r, chunk)[...]
            return 0
        lax.fori_loop(0, b * n, body, 0)
    pending = {}
    def begin(p, s):
        b, r = S.shapes[s]
        d = (p + s) % 6
        bit = bits[d]
        bo, ro = reg[p]
        if s < 4:
            src = acc.at[pl.ds(bo, b), pl.ds(pl.multiple_of(ro + (1 - bit) * r, 16), r)]
            reg[p] = [bo, ro + bit * r]
        elif s == 4:
            src = acc.at[pl.ds(bo + (1 - bit) * b, b), pl.ds(pl.multiple_of(ro, 16), r)]
            reg[p] = [bo + bit * b, ro]
        else:
            src = acc.at[pl.ds(bo, b), pl.ds(pl.multiple_of(ro, 16), r)]
        c = remote(src, recv[s].at[p], ssem.at[p, s + 1], rsem.at[p, s + 1], targets[d])
        c.start()
        pending[p, s] = c
    def finish(p, s):
        b, r = S.shapes[s]
        bo, ro = reg[p]
        c = pending.pop((p, s))
        if s == 5: c.wait()
        else:
            c.wait_recv()
            c.wait_send()
        ch = 48
        add(lambda k, rr, n: acc.at[bo + k, pl.ds(pl.multiple_of(ro + rr, 16), n)], lambda k, rr, n: recv[s].at[p, k, pl.ds(pl.multiple_of(rr, 16), n)], b, r, ch)
    vo_ref[...] = v_ref[...]
    vcopy = {}
    def vbegin(s):
        vcopy[s] = remote(vo_ref, vbuf.at[s], vss.at[s], vrs.at[s], sibling if s == 0 else targets[s - 1])
        vcopy[s].start()
    def vfinish(s):
        vcopy[s].wait()
        vo_ref[...] = vo_ref[...] + vbuf[s]
    vbegin(0)
    for p in range(6):
        cc[p].wait(); lc[p].wait()
        add(lambda k, rr, n: acc.at[p * width + k, pl.ds(pl.multiple_of(rr, 16), n)], lambda k, rr, n: corebuf.at[p * width + k, pl.ds(pl.multiple_of(rr, 16), n)], width, S.rows, 192)
        begin(p, 0)
    for s in range(6):
        vfinish(s)
        vbegin(s + 1)
        for p in range(6):
            finish(p, s)
            if s < 5: begin(p, s + 1)
            else:
                b, r = S.shapes[5]
                bo, ro = reg[p]
                l = pltpu.make_async_copy(acc.at[pl.ds(bo, b), pl.ds(pl.multiple_of(ro, 16), r)],
                                          o_ref.at[pl.ds(core * S.half + bo, b), pl.ds(pl.multiple_of(ro, 16), r)], sag.at[p, 5])
                l.start(); pending[p, "l"] = l
    vfinish(6)
    def gather(p, s):
        b, r = S.shapes[s]
        bo, ro = reg[p]
        d = (p + s) % 6
        ref = o_ref.at[pl.ds(core * S.half + bo, b), pl.ds(pl.multiple_of(ro, 16), r)]
        c = remote(ref, ref, sag.at[p, s], rag.at[p, s], targets[d])
        c.start(); pending[p, s] = c
        bit = bits[d]
        if s == 4: reg[p] = [bo - bit * b, ro]
        else: reg[p] = [bo, ro - bit * r]
    for p in range(6):
        pending.pop((p, "l")).wait()
        gather(p, 4)
    for s in range(4, -1, -1):
        for p in range(6):
            pending.pop((p, s)).wait()
            if s > 0: gather(p, s - 1)
            else:
                ref = o_ref.at[pl.ds(core * S.half + p * width, width)]
                c = remote(ref, ref, ssem.at[p, 7], rag.at[p, 5], sibling)
                c.start(); pending[p, "c"] = c
    for p in range(6):
        pending.pop((p, "c")).wait()

def all_reduce(g, v, cid=1):
    S = Stream(g.shape[0], g.shape[1])
    return pl.pallas_call(functools.partial(ar_kernel, S),
        out_shape=(jax.ShapeDtypeStruct(g.shape, g.dtype), jax.ShapeDtypeStruct(v.shape, v.dtype)),
        in_specs=[pl.BlockSpec(memory_space=pl.ANY), pl.BlockSpec(memory_space=pltpu.VMEM)],
        out_specs=(pl.BlockSpec(memory_space=pl.ANY), pl.BlockSpec(memory_space=pltpu.VMEM)),
        scratch_shapes=[pltpu.VMEM((7,) + v.shape, v.dtype), pltpu.SemaphoreType.DMA((7,)), pltpu.SemaphoreType.DMA((7,))] + S.scratch(),
        compiler_params=pltpu.CompilerParams(collective_id=cid, has_side_effects=True, vmem_limit_bytes=60*2**20))(g, v)

def widen_kernel(g_ref, up_ref, down_ref, out_ref, qkv_ref, stage, sem):
    t = pl.program_id(0)
    slot = lax.rem(t, 2)
    def cols(j): return pl.ds(pl.multiple_of(j * 768, 768), 768)
    def send(ref, s): return pltpu.make_async_copy(stage.at[s], ref, sem.at[s])
    @pl.when(t >= 2)
    def _(): send(out_ref.at[0], slot).wait()
    for b in range(6):
        stage[slot, :, b * 128:(b + 1) * 128] = g_ref[b].astype(F32)
    @pl.when(t < 4)
    def _(): send(up_ref.at[0, :, cols(t)], slot).start()
    @pl.when((t >= 4) & (t < 8))
    def _(): send(down_ref.at[0, cols(t - 4), :], slot).start()
    @pl.when(t == 8)
    def _(): send(out_ref.at[0], slot).start()
    @pl.when(t > 8)
    def _(): send(qkv_ref.at[0, :, cols(t - 9)], slot).start()
    @pl.when(t == 11)
    def _():
        send(out_ref.at[0], 0).wait()
        send(out_ref.at[0], 1).wait()

def widen(g):
    S = jax.ShapeDtypeStruct
    any_ = pl.BlockSpec(memory_space=pl.ANY)
    return pl.pallas_call(widen_kernel, grid=(12,),
        out_shape=(S((1, D, FF), F32), S((1, FF, D), F32), S((1, D, D), F32), S((1, D, 3 * D), F32)),
        in_specs=[pl.BlockSpec((6, 768, 128), lambda t: (t, 0, 0))], out_specs=(any_,) * 4,
        scratch_shapes=[pltpu.VMEM((2, 768, 768), F32), pltpu.SemaphoreType.DMA((2,))],
        compiler_params=pltpu.CompilerParams(vmem_limit_bytes=40 * 2**20))(g)


def body(hidden, text_counts, region_counts, qkv_weight, qv_bias, out_weight, out_bias, norm1_gain, norm1_bias,
         up_weight, up_bias, down_weight, down_bias, norm2_gain, norm2_bias, out_grad):
    mod = lax.axis_index("mod")
    swap = functools.partial(lax.ppermute, axis_name="mod", perm=[(0, 1), (1, 0)])
    h, og = hidden[:, 0], out_grad[:, 0]
    rh = swap(lax.dynamic_slice_in_dim(h, 3 * (1 - mod), 4))
    rog = swap(lax.dynamic_slice_in_dim(og, 4 * (1 - mod), 3))
    y, yo, ig, igo, mid, grads, vec = compute(99, h, rh, og, rog, text_counts, region_counts, qkv_weight[0], qv_bias,
        out_weight[0], out_bias, norm1_gain, norm1_bias, up_weight[0], up_bias, down_weight[0], down_bias, norm2_gain, norm2_bias)
    ry, rig = swap(yo), swap(igo)
    y = lax.dynamic_update_slice_in_dim(y, ry, 4 * (1 - mod), 0)
    ig = lax.dynamic_update_slice_in_dim(ig, rig, 3 * (1 - mod), 0)
    both = mid + lax.dynamic_index_in_dim(rig, 3 * mod, keepdims=False).astype(F32)
    ig = lax.dynamic_update_slice_in_dim(ig, both.astype(BF)[None], 3, 0)
    grads, vec = all_reduce(grads, vec)
    up, down, out, qkv = widen(grads)
    def part(name, n): return vec[:, VEC[name]:VEC[name] + n]
    return (y[:, None], ig[:, None], qkv, part("q", 1536), out, part("out", 768), part("g1", 768), part("b1", 768), up, part("up", 3072),
            down, part("down", 768), part("g2", 768), part("b2", 768))


def solution(mesh):
    rows, pairs, whole = P("batch", "mod", None, None), P("batch"), P()
    return jax.shard_map(body, mesh=mesh, in_specs=(rows, pairs, pairs) + (whole,) * 12 + (rows,),
                         out_specs=(rows, rows) + (whole,) * 12, check_vma=False)
```

```python
import functools
import math

import jax
import jax.numpy as jnp
from jax import lax
from jax.experimental import pallas as pl
from jax.experimental.pallas import tpu as pltpu
from jax.sharding import PartitionSpec as P

MESH = pl.DeviceIdType.MESH
BF, F32 = jnp.bfloat16, jnp.float32
D, FF, SLOTS = 768, 3072, 128
WHOLE = 3
OWN = (WHOLE + 1) * SLOTS
QROWS = OWN + WHOLE * SLOTS
KROWS = 2 * OWN
HALF = D // 2
EPS = 1e-6
MASKED = -1e9
LOG2E = math.log2(math.e)
SCALE = 0.125
LN_ROWS = 128
PARTS = 6
CUTS = (192, 96, 48)
RECV_AT = (0, 192, 288, 336, 384, 432)
RECV_ROWS = 480
VEC = dict(q=0, v=768, out=1536, g1=2304, b1=3072, up=3840, down=6912, g2=7680, b2=8448)
VLEN = 9216


def nn(a, b):
    return lax.dot_general(a, b, (((1,), (0,)), ((), ())), preferred_element_type=F32)


def nt(a, b):
    return lax.dot_general(a, b, (((1,), (1,)), ((), ())), preferred_element_type=F32)


def tn(a, b):
    return lax.dot_general(a, b, (((0,), (0,)), ((), ())), preferred_element_type=F32)


def gelu_pair(v):
    e = jnp.exp2(v * v * (-0.5 * LOG2E))
    d = 1.0 + (0.3275911 / math.sqrt(2.0)) * jnp.abs(v)
    t = pl.reciprocal(d, approx=True)
    t = t * (2.0 - d * t)
    poly = 0.5 * 1.061405429 * t - 0.5 * 1.453152027
    poly = ((poly * t + 0.5 * 1.421413741) * t - 0.5 * 0.284496736) * t + 0.5 * 0.254829592
    tail = poly * t * e
    cdf = jnp.where(v >= 0, 1.0 - tail, tail)
    return v * cdf, cdf + v * e * (1.0 / math.sqrt(2.0 * math.pi))


def normalize(s):
    centre = s - jnp.mean(s, -1, keepdims=True)
    r = lax.rsqrt(jnp.mean(centre * centre, -1, keepdims=True) + EPS)
    return centre * r, r


def norm_back(g, n, r):
    return r * (g - jnp.mean(g, -1, keepdims=True) - n * jnp.mean(g * n, -1, keepdims=True))


def fold(v):
    return v.reshape(v.shape[0] // 8, 8, v.shape[1]).sum(0)


def half(v, h):
    lane = lax.broadcasted_iota(jnp.int32, v.shape, 1)
    return jnp.where((lane < 64) if h == 0 else (lane >= 64), v, jnp.zeros((), BF))


def place():
    mod, batch = lax.axis_index("mod"), lax.axis_index("batch")
    return mod * 2 + lax.rem(batch // 2, 2), batch // 16, lax.rem(batch // 4, 4), lax.rem(batch, 2)


def device(x, y, z, core):
    return (x // 2, y * 16 + z * 4 + lax.rem(x, 2) * 2 + core)


def near(v):
    return v + 1 - 2 * lax.rem(v, 2)


def remote(src, dst, send, recv, target):
    return pltpu.make_async_remote_copy(src, dst, send, recv, device_id=target, device_id_type=MESH)


class Links:
    def __init__(self):
        x, y, z, core = place()
        self.targets = [device(near(x), y, z, core), device(x, near(y), z, core), device(x, y, near(z), core),
                        device(3 - x, y, z, core), device(x, 3 - y, z, core), device(x, y, 3 - z, core)]
        bits = [lax.rem((v + 1) // 2, 2) for v in (x, y, z)] + [v // 2 for v in (x, y, z)]
        self.sibling, self.core = device(x, y, z, 1 - core), core
        self.at, self.gone = [], []
        for p in range(PARTS):
            at, gone = [0], []
            for s, r in enumerate(CUTS):
                bit = bits[(p + s) % 6]
                gone.append(at[-1] + (1 - bit) * r)
                at.append(at[-1] + bit * r)
            self.at.append(at)
            self.gone.append(gone)


class Sum:
    def __init__(self, links, width, acc, core, recv, out, sems):
        self.links, self.width, self.part = links, width, width // PARTS
        self.acc_at, self.core_at, self.recv_at, self.out = acc, core, recv, out
        self.csend, self.crecv, self.ssend, self.srecv, self.gsend, self.grecv, self.fsend, self.frecv, self.local = sems

    def view(self, where, row, rows, col, cols):
        ref, r0, c0 = where
        if not isinstance(row, int):
            row = pl.multiple_of(row + r0, 16)
        else:
            row = row + r0
        return ref.at[pl.ds(row, rows), pl.ds(c0 + col, cols)]

    def tile_copy(self, send, t):
        c0 = self.core_at[2]
        cols = pl.ds(pl.multiple_of(c0 + t * 768, 128), 768)
        return remote(send.at[:, cols], self.core_at[0].at[pl.ds(self.core_at[1], HALF), cols],
                      self.csend.at[t], self.crecv.at[t], self.links.sibling)

    def acc_tile(self, t):
        ref, r0, c0 = self.acc_at
        return ref.at[pl.ds(r0, HALF), pl.ds(pl.multiple_of(c0 + t * 768, 128), 768)]

    def step_copy(self, p, s):
        col, w = p * self.part, self.part
        if s < 3:
            src = self.view(self.acc_at, self.links.gone[p][s], CUTS[s], col, w)
        else:
            src = self.view(self.acc_at, self.links.at[p][3], CUTS[2], col, w)
        dst = self.view(self.recv_at, RECV_AT[s], CUTS[min(s, 2)], col, w)
        return remote(src, dst, self.ssend.at[p], self.srecv.at[p, s], self.links.targets[(p + s) % 6])

    def add(self, p, row, rows, src, src_row):
        a = self.view(self.acc_at, row, rows, p * self.part, self.part)
        b = self.view(src, src_row, rows, p * self.part, self.part)
        n = 48
        def chunk(i, _):
            rr = pl.ds(pl.multiple_of(i * n, 16), n)
            a[rr, :] = a[rr, :] + b[rr, :]
            return 0
        if rows == n:
            a[...] = a[...] + b[...]
        else:
            lax.fori_loop(0, rows // n, chunk, 0)

    def out_view(self, p, row, rows):
        start = pl.multiple_of(self.links.core * HALF + row, 16)
        return self.out.at[pl.ds(start, rows), pl.ds(p * self.part, self.part)]

    def place_copy(self, p):
        return pltpu.make_async_copy(self.view(self.acc_at, self.links.at[p][3], CUTS[2], p * self.part, self.part),
                                     self.out_view(p, self.links.at[p][3], CUTS[2]), self.local.at[p])

    def gather_copy(self, p, s):
        row = self.links.at[p][s + 1]
        dst = self.out_view(p, row, CUTS[s])
        src = self.view(self.acc_at, row, CUTS[s], p * self.part, self.part) if s == 2 else dst
        return remote(src, dst, self.gsend.at[p], self.grecv.at[p, s], self.links.targets[(p + s) % 6])

    def pass_copy(self, p, k):
        if k == 3:
            dst = self.out_view(p, self.links.at[p][3], CUTS[2])
            src = self.view(self.acc_at, self.links.at[p][3], CUTS[2], p * self.part, self.part)
        else:
            src = dst = self.out_view(p, self.links.gone[p][k], CUTS[k])
        return remote(src, dst, self.fsend.at[p], self.frecv.at[p, k], self.links.sibling)

    def steps(self, send):
        done = 0
        for p in range(PARTS):
            need = ((p + 1) * self.part - 1) // 768
            while done <= need:
                self.tile_copy(send, done).wait()
                done += 1
            self.add(p, 0, HALF, self.core_at, 0)
            self.step_copy(p, 0).start()
        yield
        for s in range(6):
            for p in range(PARTS):
                self.step_copy(p, s).wait()
                self.add(p, self.links.at[p][min(s + 1, 3)], CUTS[min(s, 2)], self.recv_at, RECV_AT[s])
                if s < 5:
                    self.step_copy(p, s + 1).start()
                else:
                    self.place_copy(p).start()
                    self.gather_copy(p, 2).start()
                    self.pass_copy(p, 3).start()
            yield
        for s in (2, 1, 0):
            for p in range(PARTS):
                if s == 2:
                    self.place_copy(p).wait()
                self.gather_copy(p, s).wait()
                if s > 0:
                    self.gather_copy(p, s - 1).start()
                self.pass_copy(p, s + 1).wait_send()
                self.pass_copy(p, s).start()
            yield
        for p in range(PARTS):
            self.pass_copy(p, 0).wait_send()
            for k in range(4):
                self.pass_copy(p, k).wait_recv()


def sum_sems(tiles):
    dma = pltpu.SemaphoreType.DMA
    return [dma((tiles,)), dma((tiles,)), dma((PARTS,)), dma((PARTS, 6)), dma((PARTS,)), dma((PARTS, 3)),
            dma((PARTS,)), dma((PARTS, 4)), dma((PARTS,))]


SEMS = 9


def layer_kernel(hid, og, tc, rc, wqkv_h, qvb, wo_h, bo_l, g1_l, b1_l, wup_h, bup_l, wdn_h, bdn_l, g2_l, b2_l,
                 y_ref, ig_ref, down_o, up_o, out_o, qkv_o, vec,
                 x, tbuf, merged, ctx, fsum, flow, act, pre, branch, dsec, mid_recv, wqkv, wo, wup, wdn, ogv,
                 send, s1, s1recv, s2recv, bqkv, bup, small, colsum, vbuf, wsem, iosem, xs, xr, free_act, free_pre, vs, vr, *sems):
    mod, batch = lax.axis_index("mod"), lax.axis_index("batch")
    links = Links()
    partner = (1 - mod, batch)
    core = links.core
    barrier = pltpu.get_barrier_semaphore()
    for t in links.targets + [links.sibling, partner]:
        pl.semaphore_signal(barrier, inc=1, device_id=t, device_id_type=MESH)

    def pair_of(i):
        return i + mod * (6 - 2 * i)

    def given(i):
        return i + (1 - mod) * (6 - 2 * i)

    def own_count(i):
        return jnp.where(mod == 0, tc[pair_of(i)], rc[pair_of(i)])

    def other_count(i):
        return jnp.where(mod == 0, rc[pair_of(i)], tc[pair_of(i)])

    def rows_of(i, n=SLOTS):
        return pl.ds(pl.multiple_of(i * SLOTS, SLOTS), n)

    weights = [pltpu.make_async_copy(src, dst, wsem.at[k])
               for k, (src, dst) in enumerate([(wqkv_h, wqkv), (wo_h, wo), (wup_h, wup), (wdn_h, wdn)])]
    xin = [pltpu.make_async_copy(hid.at[pair_of(i)], x.at[rows_of(i)], iosem.at[i]) for i in range(4)]
    ogin = [pltpu.make_async_copy(og.at[pair_of(i)], ogv.at[rows_of(i)], iosem.at[4 + i]) for i in range(4)]
    for c in xin + weights[:1]:
        c.start()
    pl.semaphore_wait(barrier, 8)

    def x_copy(i):
        return remote(hid.at[given(i)], x.at[rows_of(i + 4)], xs.at[i], xr.at[i], partner)

    def og_copy(i):
        return remote(og.at[given(i)], ogv.at[rows_of(i + 4)], xs.at[4 + i], xr.at[4 + i], partner)
    for i in range(4):
        x_copy(i).start()
    for i in range(3):
        og_copy(i).start()
    for c in weights[1:] + ogin:
        c.start()

    bqkv[:, 0:768] = qvb[:, 0:768].astype(F32)
    bqkv[:, 768:1536] = jnp.zeros((1, 768), F32)
    bqkv[:, 1536:2304] = qvb[:, 768:1536].astype(F32)
    bup[...] = bup_l[...].astype(F32)
    for k, l in enumerate((bo_l, g1_l, b1_l, bdn_l, g2_l, b2_l)):
        small[k] = l[...].astype(F32)
    bo, g1, b1, bdn, g2, b2 = (small.at[k] for k in range(6))

    nsem = [sems[k * SEMS:(k + 1) * SEMS] for k in range(4)]
    sum_down = Sum(links, FF, (s1, 0, 0), (s1, HALF, 0), (s1recv, 0, 0), down_o, nsem[0])
    sum_up = Sum(links, FF, (act, 0, 0), (act, HALF, 0), (s2recv, 0, 0), up_o, nsem[1])
    sum_out = Sum(links, D, (pre, 0, 3 * D), (pre, HALF, 3 * D), (wup, 0, 3 * D), out_o, nsem[2])
    sum_qkv = Sum(links, 3 * D, (pre, 0, 0), (pre, HALF, 0), (wup, 0, 0), qkv_o, nsem[3])
    running = []

    def serve():
        for g in list(running):
            if next(g, 0) == 0:
                running.remove(g)

    def serve_at(t, count):
        for k in range(count):
            @pl.when(t == k)
            def _():
                serve()

    own_half, other_half = core * HALF, (1 - core) * HALF

    for c in xin + weights[:1]:
        c.wait()

    def project(first, n):
        def tile(j, _):
            cols = pl.ds(pl.multiple_of(j * 768, 768), 768)
            merged[first, cols] = (nn(x[first, :], wqkv[:, cols]) + bqkv[:, cols]).astype(BF)
            return 0
        lax.fori_loop(0, 3, tile, 0)
    project(pl.ds(0, OWN), OWN)

    def key_live(i, nq):
        r = lax.broadcasted_iota(jnp.int32, (256, nq), 0)
        return r < jnp.where(r < SLOTS, own_count(i), SLOTS + other_count(i))

    def both(ref, i, cols):
        return jnp.concatenate([ref[rows_of(i), cols], ref[rows_of(i + 4), cols]], 0)

    def queries_of(ref, i, cols, nq):
        return both(ref, i, cols) if nq == 256 else ref[rows_of(i), cols]

    def attend(i, hp, nq):
        c0 = hp * 128
        q = queries_of(merged, i, pl.ds(c0, 128), nq)
        k = both(merged, i, pl.ds(c0 + D, 128))
        v = both(merged, i, pl.ds(c0 + 2 * D, 128))
        live = key_live(i, nq)
        out = None
        for h in range(2):
            s = nt(half(k, h), q) * (SCALE * LOG2E)
            s = jnp.where(live, s, MASKED)
            e = jnp.exp2(s - jnp.max(s, 0, keepdims=True))
            p = (e * (1.0 / jnp.sum(e, 0, keepdims=True))).astype(BF)
            o = tn(p, half(v, h))
            out = o if out is None else out + o
        out = out.astype(BF)
        ctx[rows_of(i), pl.ds(c0, 128)] = out[:SLOTS]
        if nq == 256:
            ctx[rows_of(i + 4), pl.ds(c0, 128)] = out[SLOTS:]

    def forward_pair(i, nq):
        x_copy(i).wait_recv()
        project(rows_of(i + 4), SLOTS)
        for hp in range(6):
            attend(i, hp, nq)

    def forward_whole(i, _):
        forward_pair(i, 256)
        return 0
    lax.fori_loop(0, WHOLE, forward_whole, 0)
    forward_pair(WHOLE, SLOTS)

    weights[1].wait()
    fsum[...] = x[0:QROWS, :].astype(F32) + nn(ctx[...], wo[...]) + bo[...]

    def first_rows(r, _):
        rows = pl.ds(pl.multiple_of(r * LN_ROWS, LN_ROWS), LN_ROWS)
        n, _r = normalize(fsum[rows, :])
        flow[rows, :] = (n * g1[...] + b1[...]).astype(BF)
        return 0
    lax.fori_loop(0, QROWS // LN_ROWS, first_rows, 0)

    weights[2].wait()

    def up_tile(j, _):
        cols = pl.ds(pl.multiple_of(j * 768, 768), 768)
        a, d = gelu_pair(nn(flow[...], wup[:, cols]) + bup[:, cols])
        act[:, cols] = a.astype(BF)
        pre[:, cols] = d.astype(BF)
        return 0
    lax.fori_loop(0, 4, up_tile, 0)
    weights[3].wait()
    dsec[...] = nn(act[...], wdn[...]) + bdn[...]
    for c in ogin:
        c.wait()
    for i in range(3):
        og_copy(i).wait()
    for i in range(4):
        x_copy(i).wait_send()

    colsum[...] = jnp.zeros_like(colsum)

    def second_rows(r, _):
        rows = pl.ds(pl.multiple_of(r * LN_ROWS, LN_ROWS), LN_ROWS)
        count = jnp.where(r < 4, own_count(lax.rem(r, 4)), other_count(lax.rem(r, 4)))
        live = (lax.broadcasted_iota(jnp.int32, (LN_ROWS, 1), 0) < count).astype(F32)
        n, rr = normalize(fsum[rows, :])
        n, rr = normalize(n * g1[...] + b1[...] + dsec[rows, :])
        dout = ogv[rows, :].astype(F32) * live
        ogv[rows, :] = ((n * g2[...] + b2[...]) * live).astype(BF)
        colsum[0] += fold(dout * n)
        colsum[1] += fold(dout)
        ds = norm_back(dout * g2[...], n, rr)
        dsec[rows, :] = ds
        low = ds.astype(BF)
        branch[rows, :] = low
        colsum[2] += fold(low.astype(F32))
        return 0
    lax.fori_loop(0, QROWS // LN_ROWS, second_rows, 0)
    for k, name in enumerate(("g2", "b2", "down")):
        vec[:, VEC[name]:VEC[name] + 768] = jnp.sum(colsum[k], 0, keepdims=True)

    def y_local(i):
        return pltpu.make_async_copy(ogv.at[rows_of(i)], y_ref.at[pair_of(i)], iosem.at[i])

    def y_remote(i):
        return remote(ogv.at[rows_of(i + 4)], y_ref.at[pair_of(i)], xs.at[i], xr.at[7 + i], partner)
    for i in range(4):
        y_local(i).start()
    for i in range(3):
        y_remote(i).start()

    def down_tile(t, _):
        def rows(first):
            return pl.ds(pl.multiple_of(t * 768 + first, 128), HALF)
        cols = pl.ds(pl.multiple_of(t * 768, 768), 768)
        send[:, cols] = tn(act[:, rows(other_half)], branch[...]).astype(BF)
        sum_down.tile_copy(send, t).start()
        sum_down.acc_tile(t)[...] = tn(act[:, rows(own_half)], branch[...]).astype(BF)
        return 0
    lax.fori_loop(0, 4, down_tile, 0)
    pl.semaphore_signal(free_act, inc=1, device_id=links.sibling, device_id_type=MESH)
    running.append(sum_down.steps(send))
    serve()

    tbuf[:, 0:QROWS] = flow[...].T
    pl.semaphore_wait(free_act, 1)

    def rows_half(first):
        return pl.ds(pl.multiple_of(first, 128), HALF)

    def gelu_tile(j, _):
        cols = pl.ds(pl.multiple_of(j * 768, 768), 768)
        low = (nt(branch[...], wdn[cols, :]) * pre[:, cols].astype(F32)).astype(BF)
        pre[:, cols] = low
        vec[:, pl.ds(pl.multiple_of(VEC["up"] + j * 768, 768), 768)] = jnp.sum(low.astype(F32), 0, keepdims=True)
        send[:, cols] = nn(tbuf[rows_half(other_half), 0:QROWS], low).astype(BF)
        sum_up.tile_copy(send, j).start()
        sum_up.acc_tile(j)[...] = nn(tbuf[rows_half(own_half), 0:QROWS], low).astype(BF)
        serve_at(j, 4)
        return 0
    lax.fori_loop(0, 4, gelu_tile, 0)
    running.append(sum_up.steps(send))
    serve()

    dsec[...] += nt(pre[...], wup[...])
    for t in links.targets + [links.sibling]:
        pl.semaphore_signal(free_pre, inc=1, device_id=t, device_id_type=MESH)
    serve()
    colsum[...] = jnp.zeros_like(colsum)

    def first_back(r, _):
        rows = pl.ds(pl.multiple_of(r * LN_ROWS, LN_ROWS), LN_ROWS)
        g = dsec[rows, :]
        n, rr = normalize(fsum[rows, :])
        colsum[0] += fold(g * n)
        colsum[1] += fold(g)
        df = norm_back(g * g1[...], n, rr)
        dsec[rows, :] = df
        low = df.astype(BF)
        branch[rows, :] = low
        colsum[2] += fold(low.astype(F32))
        return 0
    lax.fori_loop(0, QROWS // LN_ROWS, first_back, 0)
    for k, name in enumerate(("g1", "b1", "out")):
        vec[:, VEC[name]:VEC[name] + 768] = jnp.sum(colsum[k], 0, keepdims=True)
    serve()
    flow[...] = nt(branch[...], wo[...]).astype(BF)
    pl.semaphore_wait(free_pre, 7)
    send[:, 3 * D:] = tn(ctx[:, rows_half(other_half)], branch[...]).astype(BF)
    out_copy = remote(send.at[:, pl.ds(3 * D, D)], pre.at[pl.ds(HALF, HALF), pl.ds(3 * D, D)],
                      sum_out.csend.at[0], sum_out.crecv.at[0], links.sibling)
    out_copy.start()
    sum_out.acc_tile(0)[...] = tn(ctx[:, rows_half(own_half)], branch[...]).astype(BF)
    running.append(sum_out.steps(send))
    serve()

    def attend_back(i, hp, nq):
        c0 = pl.multiple_of(hp * 128, 128)
        qs, ks, vs_ = (pl.ds(c0 + D * m, 128) for m in range(3))
        q, dc = queries_of(merged, i, qs, nq), queries_of(flow, i, pl.ds(c0, 128), nq)
        k, v = both(merged, i, ks), both(merged, i, vs_)
        live = key_live(i, nq)
        dq = dk = dv = None
        for h in range(2):
            kh = half(k, h)
            s = nt(kh, q) * (SCALE * LOG2E)
            s = jnp.where(live, s, MASKED)
            e = jnp.exp2(s - jnp.max(s, 0, keepdims=True))
            p = e * (1.0 / jnp.sum(e, 0, keepdims=True))
            dp = nt(half(v, h), dc)
            ds = (p * (dp - jnp.sum(p * dp, 0, keepdims=True))).astype(BF)
            a, b, c = nn(p.astype(BF), half(dc, h)), nn(ds, half(q, h)), tn(ds, kh)
            dv, dk, dq = (a, b, c) if h == 0 else (dv + a, dk + b, dq + c)
        dq, dk, dv = (dq * SCALE).astype(BF), (dk * SCALE).astype(BF), dv.astype(BF)
        merged[rows_of(i), qs] = dq[:SLOTS]
        merged[rows_of(i + 4), qs] = dq[SLOTS:] if nq == 256 else jnp.zeros((SLOTS, 128), BF)
        merged[rows_of(i), ks] = dk[:SLOTS]
        merged[rows_of(i + 4), ks] = dk[SLOTS:]
        merged[rows_of(i), vs_] = dv[:SLOTS]
        merged[rows_of(i + 4), vs_] = dv[SLOTS:]

    def back_whole(t, _):
        for u in range(3):
            attend_back(t // 2, lax.rem(t, 2) * 3 + u, 256)
        serve_at(t, 2 * WHOLE)
        return 0
    lax.fori_loop(0, 2 * WHOLE, back_whole, 0)

    def back_middle(t, _):
        for u in range(3):
            attend_back(WHOLE, t * 3 + u, SLOTS)
        serve_at(t, 2)
        return 0
    lax.fori_loop(0, 2, back_middle, 0)

    tbuf[...] = x[...].T

    def qkv_tile(j, _):
        cols = pl.ds(pl.multiple_of(j * 768, 768), 768)
        send[:, cols] = nn(tbuf[rows_half(other_half), :], merged[:, cols]).astype(BF)
        sum_qkv.tile_copy(send, j).start()
        sum_qkv.acc_tile(j)[...] = nn(tbuf[rows_half(own_half), :], merged[:, cols]).astype(BF)
        @pl.when(j != 1)
        def _():
            vec[:, pl.ds(pl.multiple_of((j // 2) * 768, 768), 768)] = jnp.sum(merged[:, cols].astype(F32), 0, keepdims=True)
        serve_at(j, 3)
        return 0
    lax.fori_loop(0, 3, qkv_tile, 0)

    def vec_copy(s):
        return remote(vec, vbuf.at[s], vs.at[s], vr.at[s], links.sibling if s == 0 else links.targets[s - 1])

    def vec_steps():
        vec_copy(0).start()
        yield
        for s in range(7):
            vec_copy(s).wait()
            vec[...] = vec[...] + vbuf[s]
            if s < 6:
                vec_copy(s + 1).start()
            yield
    running.append(sum_qkv.steps(send))
    running.append(vec_steps())
    serve()

    def y_done():
        for i in range(4):
            y_local(i).wait()
        for i in range(3):
            y_remote(i).wait()
    y_done()
    g = nt(merged[OWN:, :], wqkv[...])
    ogv[0:384, :] = (g[0:384] + dsec[OWN:, :]).astype(BF)
    ogv[384:512, :] = g[384:].astype(BF)

    def ig_remote(i):
        dst = ig_ref.at[pair_of(i)] if i < 3 else mid_recv
        return remote(ogv.at[pl.ds(i * SLOTS, SLOTS)], dst, xs.at[i], xr.at[10 + i], partner)
    for i in range(4):
        ig_remote(i).start()
    serve()
    g = nt(merged[0:OWN, :], wqkv[...]) + dsec[0:OWN, :]
    x[0:384, :] = g[0:384].astype(BF)
    dsec[0:SLOTS, :] = g[384:]

    def ig_local(i):
        return pltpu.make_async_copy(x.at[pl.ds(i * SLOTS, SLOTS)], ig_ref.at[pair_of(i)], iosem.at[i])
    for i in range(3):
        ig_local(i).start()
    serve()
    serve()
    serve()
    ig_remote(3).wait()
    x[384:512, :] = (dsec[0:SLOTS, :] + mid_recv[...].astype(F32)).astype(BF)
    ig_local(3).start()
    while running:
        serve()
    for i in range(4):
        ig_local(i).wait()
        if i < 3:
            ig_remote(i).wait()


def layer(*args):
    any_, vm, sm = (pl.BlockSpec(memory_space=m) for m in (pl.ANY, pltpu.VMEM, pltpu.SMEM))
    S, V, dma = jax.ShapeDtypeStruct, pltpu.VMEM, pltpu.SemaphoreType.DMA
    sems = []
    for tiles in (4, 4, 1, 3):
        sems += sum_sems(tiles)
    return pl.pallas_call(
        layer_kernel,
        out_shape=(S((7, SLOTS, D), BF), S((7, SLOTS, D), BF), S((D, FF), BF), S((D, FF), BF), S((D, D), BF),
                   S((D, 3 * D), BF), S((1, VLEN), F32)),
        in_specs=[any_] * 2 + [sm] * 2 + [any_, vm, any_, vm, vm, vm, any_, vm, any_, vm, vm, vm],
        out_specs=(any_,) * 6 + (vm,),
        scratch_shapes=[
            V((KROWS, D), BF), V((D, KROWS), BF), V((KROWS, 3 * D), BF), V((QROWS, D), BF), V((QROWS, D), F32),
            V((QROWS, D), BF), V((QROWS, FF), BF), V((QROWS, FF), BF), V((QROWS, D), BF), V((QROWS, D), F32),
            V((SLOTS, D), BF), V((D, 3 * D), BF), V((D, D), BF), V((D, FF), BF), V((FF, D), BF), V((QROWS, D), BF),
            V((HALF, FF), BF), V((D, FF), BF), V((RECV_ROWS, FF), BF), V((RECV_ROWS, FF), BF),
            V((1, 3 * D), F32), V((1, FF), F32), V((6, 1, D), F32), V((3, 8, D), F32), V((7, 1, VLEN), F32),
            dma((4,)), dma((8,)), dma((7,)), dma((14,)), pltpu.SemaphoreType.REGULAR, pltpu.SemaphoreType.REGULAR,
            dma((7,)), dma((7,))] + sems,
        compiler_params=pltpu.CompilerParams(collective_id=1, has_side_effects=True, vmem_limit_bytes=63 * 2**20),
    )(*args)


def widen_kernel(down_ref, up_ref, out_ref, qkv_ref, down_o, up_o, out_o, qkv_o, buf, stage, rsem, wsem):
    tiles = []
    for t in range(4):
        tiles.append((down_ref.at[:, pl.ds(t * D, D)], down_o.at[0, pl.ds(t * D, D), :]))
    for t in range(4):
        tiles.append((up_ref.at[:, pl.ds(t * D, D)], up_o.at[0, :, pl.ds(t * D, D)]))
    tiles.append((out_ref, out_o.at[0]))
    for t in range(3):
        tiles.append((qkv_ref.at[:, pl.ds(t * D, D)], qkv_o.at[0, :, pl.ds(t * D, D)]))
    n = len(tiles)

    def read(t):
        return pltpu.make_async_copy(tiles[t][0], buf.at[t % 4], rsem.at[t % 4])

    def write(t):
        return pltpu.make_async_copy(stage.at[t % 3], tiles[t][1], wsem.at[t % 3])
    for t in range(3):
        read(t).start()
    for t in range(n):
        if t + 3 < n:
            read(t + 3).start()
        read(t).wait()
        if t >= 3:
            write(t - 3).wait()

        def chunk(r, _):
            rows = pl.ds(pl.multiple_of(r * 64, 64), 64)
            stage[t % 3, rows, :] = buf[t % 4, rows, :].astype(F32)
            return 0
        lax.fori_loop(0, D // 64, chunk, 0)
        write(t).start()
    for t in range(n - 3, n):
        write(t).wait()


def widen(*args):
    S, dma = jax.ShapeDtypeStruct, pltpu.SemaphoreType.DMA
    any_ = pl.BlockSpec(memory_space=pl.ANY)
    return pl.pallas_call(
        widen_kernel,
        out_shape=(S((1, FF, D), F32), S((1, D, FF), F32), S((1, D, D), F32), S((1, D, 3 * D), F32)),
        in_specs=[any_] * 4, out_specs=(any_,) * 4,
        scratch_shapes=[pltpu.VMEM((4, D, D), BF), pltpu.VMEM((3, D, D), F32), dma((4,)), dma((3,))],
        compiler_params=pltpu.CompilerParams(vmem_limit_bytes=40 * 2**20),
    )(*args)


def body(hidden, text_counts, region_counts, qkv_weight, qv_bias, out_weight, out_bias, norm1_gain, norm1_bias,
         up_weight, up_bias, down_weight, down_bias, norm2_gain, norm2_bias, out_grad):
    y, ig, down, up, out, qkv, vec = layer(
        hidden[:, 0], out_grad[:, 0], text_counts, region_counts, qkv_weight[0], qv_bias, out_weight[0], out_bias,
        norm1_gain, norm1_bias, up_weight[0], up_bias, down_weight[0], down_bias, norm2_gain, norm2_bias)
    down, up, out, qkv = widen(down, up, out, qkv)

    def piece(name, n):
        return vec[:, VEC[name]:VEC[name] + n]
    return (y[:, None], ig[:, None], qkv, piece("q", 1536), out, piece("out", 768), piece("g1", 768), piece("b1", 768),
            up, piece("up", 3072), down, piece("down", 768), piece("g2", 768), piece("b2", 768))


def solution(mesh):
    rows, pairs, whole = P("batch", "mod", None, None), P("batch"), P()
    return jax.shard_map(body, mesh=mesh, in_specs=(rows, pairs, pairs) + (whole,) * 12 + (rows,),
                         out_specs=(rows, rows) + (whole,) * 12, check_vma=False)
```

```python
import functools
import math

import jax
import jax.numpy as jnp
from jax import lax
from jax.experimental import pallas as pl
from jax.experimental.pallas import tpu as pltpu
from jax.sharding import PartitionSpec as P

MESH = pl.DeviceIdType.MESH
BF, F32 = jnp.bfloat16, jnp.float32
D, FF, SLOTS = 768, 3072, 128
WHOLE = 3
OWN = (WHOLE + 1) * SLOTS
QROWS = OWN + WHOLE * SLOTS
KROWS = 2 * OWN
HALF = D // 2
EPS = 1e-6
MASKED = -1e9
LOG2E = math.log2(math.e)
SCALE = 0.125
LN_ROWS = 128
PARTS = 6
CUTS = (192, 96, 48)
RECV_AT = (0, 192, 288, 336, 384, 432)
RECV_ROWS = 480
QUARTER = HALF // 4
VEC = dict(out=0, g1=1, b1=2, up=3, down=7, g2=8, b2=9)
VROWS = 16


def nn(a, b):
    return lax.dot_general(a, b, (((1,), (0,)), ((), ())), preferred_element_type=F32)


def nt(a, b):
    return lax.dot_general(a, b, (((1,), (1,)), ((), ())), preferred_element_type=F32)


def tn(a, b):
    return lax.dot_general(a, b, (((0,), (0,)), ((), ())), preferred_element_type=F32)


def gelu_pair(v):
    e = jnp.exp2(v * v * (-0.5 * LOG2E))
    d = 1.0 + (0.3275911 / math.sqrt(2.0)) * jnp.abs(v)
    t = pl.reciprocal(d, approx=True)
    t = t * (2.0 - d * t)
    poly = 0.5 * 1.061405429 * t - 0.5 * 1.453152027
    poly = ((poly * t + 0.5 * 1.421413741) * t - 0.5 * 0.284496736) * t + 0.5 * 0.254829592
    tail = poly * t * e
    cdf = jnp.where(v >= 0, 1.0 - tail, tail)
    return v * cdf, cdf + v * e * (1.0 / math.sqrt(2.0 * math.pi))


def normalize(s):
    centre = s - jnp.mean(s, -1, keepdims=True)
    r = lax.rsqrt(jnp.mean(centre * centre, -1, keepdims=True) + EPS)
    return centre * r, r


def norm_back(g, n, r):
    return r * (g - jnp.mean(g, -1, keepdims=True) - n * jnp.mean(g * n, -1, keepdims=True))


def fold(v):
    return v.reshape(v.shape[0] // 8, 8, v.shape[1]).sum(0)


def half(v, h):
    lane = lax.broadcasted_iota(jnp.int32, v.shape, 1)
    return jnp.where((lane < 64) if h == 0 else (lane >= 64), v, jnp.zeros((), BF))


def place():
    mod, batch = lax.axis_index("mod"), lax.axis_index("batch")
    return mod * 2 + lax.rem(batch // 2, 2), batch // 16, lax.rem(batch // 4, 4), lax.rem(batch, 2)


def device(x, y, z, core):
    return (x // 2, y * 16 + z * 4 + lax.rem(x, 2) * 2 + core)


def near(v):
    return v + 1 - 2 * lax.rem(v, 2)


def remote(src, dst, send, recv, target):
    return pltpu.make_async_remote_copy(src, dst, send, recv, device_id=target, device_id_type=MESH)


class Links:
    def __init__(self):
        x, y, z, core = place()
        self.targets = [device(near(x), y, z, core), device(x, near(y), z, core), device(x, y, near(z), core),
                        device(3 - x, y, z, core), device(x, 3 - y, z, core), device(x, y, 3 - z, core)]
        bits = [lax.rem((v + 1) // 2, 2) for v in (x, y, z)] + [v // 2 for v in (x, y, z)]
        self.sibling, self.core = device(x, y, z, 1 - core), core
        self.coords = [x, y, z]
        self.across = [self.along(a, 2) for a in range(3)]
        self.bits = bits

    def along(self, axis, d):
        place_ = list(self.coords)
        place_[axis] = lax.rem(place_[axis] + d, 4)
        return device(*place_, self.core)


EVEN = [[(p + s) % 6 for s in range(6)] for p in range(6)]
SPARE_X = [[1, 2, 4, 5, 0, 3], [4, 5, 1, 2, 3, 0], [2, 4, 5, 1, 0, 3], [5, 1, 2, 4, 3, 0]]


class Sum:
    def __init__(self, links, width, routes, acc, core, recv, out, sems):
        self.links, self.routes, self.parts, self.part = links, routes, len(routes), width // len(routes)
        self.at, self.gone = [], []
        for route in routes:
            at, gone = [0], []
            for s, r in enumerate(CUTS):
                bit = links.bits[route[s]]
                gone.append(at[-1] + (1 - bit) * r)
                at.append(at[-1] + bit * r)
            self.at.append(at)
            self.gone.append(gone)
        self.acc_at, self.core_at, self.recv_at, self.out = acc, core, recv, out
        self.csend, self.crecv, self.ssend, self.srecv, self.gsend, self.grecv, self.fsend, self.frecv, self.local = sems

    def view(self, where, row, rows, col, cols):
        ref, r0, c0 = where
        if not isinstance(row, int):
            row = pl.multiple_of(row + r0, 16)
        else:
            row = row + r0
        return ref.at[pl.ds(row, rows), pl.ds(c0 + col, cols)]

    def tile_copy(self, send, t):
        c0 = self.core_at[2]
        cols = pl.ds(pl.multiple_of(c0 + t * 768, 128), 768)
        return remote(send.at[:, cols], self.core_at[0].at[pl.ds(self.core_at[1], HALF), cols],
                      self.csend.at[t], self.crecv.at[t], self.links.sibling)

    def acc_tile(self, t):
        ref, r0, c0 = self.acc_at
        return ref.at[pl.ds(r0, HALF), pl.ds(pl.multiple_of(c0 + t * 768, 128), 768)]

    def step_copy(self, p, s):
        col, w = p * self.part, self.part
        if s < 3:
            src = self.view(self.acc_at, self.gone[p][s], CUTS[s], col, w)
        else:
            src = self.view(self.acc_at, self.at[p][3], CUTS[2], col, w)
        dst = self.view(self.recv_at, RECV_AT[s], CUTS[min(s, 2)], col, w)
        return remote(src, dst, self.ssend.at[p], self.srecv.at[p, s], self.links.targets[self.routes[p][s]])

    def add(self, p, row, rows, src, src_row):
        a = self.view(self.acc_at, row, rows, p * self.part, self.part)
        b = self.view(src, src_row, rows, p * self.part, self.part)
        n = 48
        def chunk(i, _):
            rr = pl.ds(pl.multiple_of(i * n, 16), n)
            a[rr, :] = a[rr, :] + b[rr, :]
            return 0
        if rows == n:
            a[...] = a[...] + b[...]
        else:
            lax.fori_loop(0, rows // n, chunk, 0)

    def out_view(self, p, row, rows):
        start = pl.multiple_of(self.links.core * HALF + row, 16)
        return self.out.at[pl.ds(start, rows), pl.ds(p * self.part, self.part)]

    def place_copy(self, p):
        return pltpu.make_async_copy(self.view(self.acc_at, self.at[p][3], CUTS[2], p * self.part, self.part),
                                     self.out_view(p, self.at[p][3], CUTS[2]), self.local.at[p])

    def gather_copy(self, p, s):
        row = self.at[p][s + 1]
        dst = self.out_view(p, row, CUTS[s])
        src = self.view(self.acc_at, row, CUTS[s], p * self.part, self.part) if s == 2 else dst
        return remote(src, dst, self.gsend.at[p], self.grecv.at[p, s], self.links.targets[self.routes[p][s]])

    def pass_copy(self, p, k):
        if k == 3:
            dst = self.out_view(p, self.at[p][3], CUTS[2])
            src = self.view(self.acc_at, self.at[p][3], CUTS[2], p * self.part, self.part)
        else:
            src = dst = self.out_view(p, self.gone[p][k], CUTS[k])
        return remote(src, dst, self.fsend.at[p], self.frecv.at[p, k], self.links.sibling)

    count = 11

    def step(self, k, send):
        if k == 0:
            done = 0
            for p in range(self.parts):
                need = ((p + 1) * self.part - 1) // 768
                while done <= need:
                    self.tile_copy(send, done).wait()
                    done += 1
                self.add(p, 0, HALF, self.core_at, 0)
                self.step_copy(p, 0).start()
        elif k <= 6:
            s = k - 1
            for p in range(self.parts):
                self.step_copy(p, s).wait()
                self.add(p, self.at[p][min(s + 1, 3)], CUTS[min(s, 2)], self.recv_at, RECV_AT[s])
                if s < 5:
                    self.step_copy(p, s + 1).start()
                else:
                    self.place_copy(p).start()
                    self.gather_copy(p, 2).start()
                    self.pass_copy(p, 3).start()
        elif k <= 9:
            s = 9 - k
            for p in range(self.parts):
                if s == 2:
                    self.place_copy(p).wait()
                self.gather_copy(p, s).wait()
                if s > 0:
                    self.gather_copy(p, s - 1).start()
                self.pass_copy(p, s + 1).wait_send()
                self.pass_copy(p, s).start()
        else:
            for p in range(self.parts):
                self.pass_copy(p, 0).wait_send()
                for k in range(4):
                    self.pass_copy(p, k).wait_recv()


class VectorSum:
    count = 8

    def __init__(self, links, vec, slots, sems):
        self.links, self.vec, self.slots = links, vec, slots
        self.ssem, self.rsem = sems

    def copy(self, s):
        return remote(self.vec, self.slots.at[pl.ds(s * VROWS, VROWS)], self.ssem.at[s], self.rsem.at[s],
                      self.links.sibling if s == 0 else self.links.targets[s - 1])

    def step(self, k, send):
        if k > 0:
            self.copy(k - 1).wait()
            self.vec[...] = self.vec[...] + self.slots[(k - 1) * VROWS:k * VROWS, :]
        if k < 7:
            self.copy(k).start()


class AxisSum:
    count = 5

    def __init__(self, links, vec, slots, first, sems):
        self.links, self.vec, self.slots, self.first = links, vec, slots, first
        self.ssem, self.rsem = sems

    def slot(self, s, k):
        return self.slots.at[pl.ds(pl.multiple_of(self.first + (s * 4 + k) * 8, 8), 8)]

    def copy(self, s, d):
        if s == 0:
            return remote(self.vec, self.slot(0, 0), self.ssem.at[0], self.rsem.at[0, 0], self.links.sibling)
        return remote(self.vec, self.slot(s, self.links.coords[s - 1]), self.ssem.at[d], self.rsem.at[s, d],
                      self.links.along(s - 1, d))

    def step(self, k, send):
        if k == 1:
            self.copy(0, 0).wait()
            self.vec[...] = self.vec[...] + self.slot(0, 0)[...]
        elif k > 1:
            self.slot(k - 1, self.links.coords[k - 2])[...] = self.vec[...]
            for d in (1, 3, 2):
                self.copy(k - 1, d).wait()
            total = self.slot(k - 1, 0)[...]
            for i in range(1, 4):
                total = total + self.slot(k - 1, i)[...]
            self.vec[...] = total
        if k < 4:
            for d in (2, 1, 3) if k else (0,):
                self.copy(k, d).start()


def sum_sems(tiles):
    dma = pltpu.SemaphoreType.DMA
    return [dma((tiles,)), dma((tiles,)), dma((PARTS,)), dma((PARTS, 6)), dma((PARTS,)), dma((PARTS, 3)),
            dma((PARTS,)), dma((PARTS, 4)), dma((PARTS,))]


def layer_kernel(hid, og, tc, rc, wqkv_h, qvb, wo_h, bo_l, g1_l, b1_l, wup_h, bup_l, wdn_h, bdn_l, g2_l, b2_l,
                 y_ref, ig_ref, down_o, up_o, out_o, qkv_o, vec, vec_qv,
                 x, merged, ctx, fsum, flow, act, pre, branch, dsec, wqkv, wo, wup, wdn, ogv,
                 send, s1, s1recv, s2recv, bqkv, bup, small, colsum, lse, wsem, iosem, xs, xr, free_act, free_pre, vs, vr, qs_sem, qr_sem, *sems):
    mod, batch = lax.axis_index("mod"), lax.axis_index("batch")
    links = Links()
    partner = (1 - mod, batch)
    core = links.core
    barrier = pltpu.get_barrier_semaphore()
    reached = links.targets + links.across + [links.sibling]
    for t in reached:
        pl.semaphore_signal(barrier, inc=1, device_id=t, device_id_type=MESH)

    def pair_of(i):
        return i + mod * (6 - 2 * i)

    def given(i):
        return i + (1 - mod) * (6 - 2 * i)

    def own_count(i):
        return jnp.where(mod == 0, tc[pair_of(i)], rc[pair_of(i)])

    def other_count(i):
        return jnp.where(mod == 0, rc[pair_of(i)], tc[pair_of(i)])

    def rows_of(i, n=SLOTS):
        return pl.ds(pl.multiple_of(i * SLOTS, SLOTS), n)

    weights = [pltpu.make_async_copy(src, dst, wsem.at[k])
               for k, (src, dst) in enumerate([(wqkv_h, wqkv), (wo_h, wo), (wup_h, wup), (wdn_h, wdn)])]
    xin = [pltpu.make_async_copy(hid.at[pair_of(i)], x.at[rows_of(i)], iosem.at[i]) for i in range(4)]
    ogin = [pltpu.make_async_copy(og.at[pair_of(i)], ogv.at[rows_of(i)], iosem.at[4 + i]) for i in range(4)]
    for c in xin + weights[:1]:
        c.start()
    pl.semaphore_wait(barrier, len(reached))

    def x_copy(i):
        return remote(hid.at[given(i)], x.at[rows_of(i + 4)], xs.at[i], xr.at[i], partner)

    def og_copy(i):
        return remote(og.at[given(i)], ogv.at[rows_of(i + 4)], xs.at[4 + i], xr.at[4 + i], partner)
    for i in range(4):
        x_copy(i).start()
    for i in range(3):
        og_copy(i).start()
    for c in weights[1:] + ogin:
        c.start()

    bqkv[:, 0:768] = qvb[:, 0:768].astype(F32)
    bqkv[:, 768:1536] = jnp.zeros((1, 768), F32)
    bqkv[:, 1536:2304] = qvb[:, 768:1536].astype(F32)
    bup[...] = bup_l[...].astype(F32)
    for k, l in enumerate((bo_l, g1_l, b1_l, bdn_l, g2_l, b2_l)):
        small[k] = l[...].astype(F32)
    bo, g1, b1, bdn, g2, b2 = (small.at[k] for k in range(6))

    left = list(sems)

    def take(n):
        out = left[:n]
        del left[:n]
        return out
    sum_down = Sum(links, FF, SPARE_X, (s1, 0, 0), (s1, HALF, 0), (s1recv, 0, 0), down_o, take(9))
    sum_up = Sum(links, FF, SPARE_X, (act, 0, 0), (act, HALF, 0), (s2recv, 0, 0), up_o, take(9))
    sum_out = Sum(links, D, EVEN, (pre, 0, 3 * D), (pre, HALF, 3 * D), (wup, 0, 3 * D), out_o, take(9))
    recv = [(wup, 0, 0), (wup, 0, D), (wup, 0, 2 * D)]
    sum_qkv = [Sum(links, D, EVEN, (pre, 0, k * D), (pre, HALF, k * D), recv[k], qkv_o.at[k], take(9)) for k in range(3)]
    sum_vec = VectorSum(links, vec, fsum, (vs, vr))
    sum_qv = AxisSum(links, vec_qv, fsum, 7 * VROWS, (qs_sem, qr_sem))
    tail = ["tail" + str(k) for k in range(10)]
    late = ["mid0", "end0", "mid1", "end1", "mid2", "end2"] + tail
    when = [(sum_down, ["down", "gelu3", "first", "out"] + late), (sum_up, ["up", "out"] + late),
            (sum_out, ["out"] + late[1:]), (sum_vec, ["out"] + late[1:]), (sum_qkv[0], late[1:]), (sum_qkv[1], late[3:]),
            (sum_qkv[2], late[5:]), (sum_qv, late[5:])]

    plan = {}
    for s, places in when:
        for k in range(s.count):
            plan.setdefault(places[k], []).append((s, k))

    def serve(name):
        for s, k in plan.get(name, []):
            s.step(k, send)

    def serve_at(name, t, values):
        for k in values:
            @pl.when(t == k)
            def _():
                serve(name + str(k))

    own_half, other_half = core * HALF, (1 - core) * HALF

    for c in xin + weights[:1]:
        c.wait()

    def project(first, n):
        def tile(j, _):
            cols = pl.ds(pl.multiple_of(j * 768, 768), 768)
            merged[first, cols] = (nn(x[first, :], wqkv[:, cols]) + bqkv[:, cols]).astype(BF)
            return 0
        lax.fori_loop(0, 3, tile, 0)
    project(pl.ds(0, OWN), OWN)

    def key_live(i, nq):
        r = lax.broadcasted_iota(jnp.int32, (256, nq), 0)
        return r < jnp.where(r < SLOTS, own_count(i), SLOTS + other_count(i))

    def both(ref, i, cols):
        return jnp.concatenate([ref[rows_of(i), cols], ref[rows_of(i + 4), cols]], 0)

    def queries_of(ref, i, cols, nq):
        return both(ref, i, cols) if nq == 256 else ref[rows_of(i), cols]

    def lse_row(i, head, b):
        return pl.ds((i * 12 + head) * 2 + b, 1)

    def attend(i, hp, nq):
        c0 = hp * 128
        q = queries_of(merged, i, pl.ds(c0, 128), nq)
        k = both(merged, i, pl.ds(c0 + D, 128))
        v = both(merged, i, pl.ds(c0 + 2 * D, 128))
        live = key_live(i, nq)
        out = None
        for h in range(2):
            s = jnp.where(live, nt(half(k, h), q) * (SCALE * LOG2E), MASKED)
            top = jnp.max(s, 0, keepdims=True)
            e = jnp.exp2(s - top)
            total = jnp.sum(e, 0, keepdims=True)
            row = top + jnp.log2(total)
            for b in range(nq // SLOTS):
                lse[lse_row(i, hp * 2 + h, b), :] = row[:, b * SLOTS:(b + 1) * SLOTS]
            o = tn((e * (1.0 / total)).astype(BF), half(v, h))
            out = o if h == 0 else out + o
        for b in range(nq // SLOTS):
            ctx[rows_of(i + 4 * b), pl.ds(c0, 128)] = out[b * SLOTS:(b + 1) * SLOTS].astype(BF)

    def forward_pair(i, nq):
        x_copy(i).wait_recv()
        project(rows_of(i + 4), SLOTS)
        for hp in range(6):
            attend(i, hp, nq)

    def forward_whole(i, _):
        forward_pair(i, 256)
        return 0
    lax.fori_loop(0, WHOLE, forward_whole, 0)
    forward_pair(WHOLE, SLOTS)

    weights[1].wait()
    fsum[...] = x[0:QROWS, :].astype(F32) + nn(ctx[...], wo[...]) + bo[...]

    def first_rows(r, _):
        rows = pl.ds(pl.multiple_of(r * LN_ROWS, LN_ROWS), LN_ROWS)
        n, _r = normalize(fsum[rows, :])
        flow[rows, :] = (n * g1[...] + b1[...]).astype(BF)
        return 0
    lax.fori_loop(0, QROWS // LN_ROWS, first_rows, 0)

    weights[2].wait()

    def up_tile(j, _):
        cols = pl.ds(pl.multiple_of(j * 768, 768), 768)
        a, d = gelu_pair(nn(flow[...], wup[:, cols]) + bup[:, cols])
        act[:, cols] = a.astype(BF)
        pre[:, cols] = d.astype(BF)
        return 0
    lax.fori_loop(0, 4, up_tile, 0)
    weights[3].wait()
    dsec[...] = nn(act[...], wdn[...]) + bdn[...]
    for c in ogin:
        c.wait()
    for i in range(3):
        og_copy(i).wait()
    for i in range(4):
        x_copy(i).wait_send()

    vec[...] = jnp.zeros_like(vec)
    vec_qv[...] = jnp.zeros_like(vec_qv)
    colsum[...] = jnp.zeros_like(colsum)

    counts = [own_count(i) for i in range(4)] + [other_count(i) for i in range(3)]

    def second_rows(r, _):
        rows = pl.ds(pl.multiple_of(r * LN_ROWS, LN_ROWS), LN_ROWS)
        place_ = lax.broadcasted_iota(jnp.int32, (LN_ROWS, 1), 0) + r * LN_ROWS
        live = jnp.zeros((LN_ROWS, 1), F32)
        for k, count in enumerate(counts):
            live = jnp.where((place_ >= k * SLOTS) & (place_ < k * SLOTS + count), 1.0, live)
        n, rr = normalize(fsum[rows, :])
        n, rr = normalize(n * g1[...] + b1[...] + dsec[rows, :])
        dout = ogv[rows, :].astype(F32) * live
        ogv[rows, :] = ((n * g2[...] + b2[...]) * live).astype(BF)
        colsum[0] += fold(dout * n)
        colsum[1] += fold(dout)
        ds = norm_back(dout * g2[...], n, rr)
        dsec[rows, :] = ds
        low = ds.astype(BF)
        branch[rows, :] = low
        colsum[2] += fold(low.astype(F32))
        return 0
    lax.fori_loop(0, QROWS // LN_ROWS, second_rows, 0)
    for k, name in enumerate(("g2", "b2", "down")):
        vec[VEC[name]:VEC[name] + 1, :] = jnp.sum(colsum[k], 0, keepdims=True)

    def y_local(i):
        return pltpu.make_async_copy(ogv.at[rows_of(i)], y_ref.at[pair_of(i)], iosem.at[i])

    def y_remote(i):
        return remote(ogv.at[rows_of(i + 4)], y_ref.at[pair_of(i)], xs.at[i], xr.at[7 + i], partner)
    for i in range(4):
        y_local(i).start()
    for i in range(3):
        y_remote(i).start()

    def down_tile(t, _):
        def rows(first):
            return pl.ds(pl.multiple_of(t * 768 + first, 128), HALF)
        cols = pl.ds(pl.multiple_of(t * 768, 768), 768)
        send[:, cols] = tn(act[:, rows(other_half)], branch[...]).astype(BF)
        sum_down.tile_copy(send, t).start()
        sum_down.acc_tile(t)[...] = tn(act[:, rows(own_half)], branch[...]).astype(BF)
        return 0
    lax.fori_loop(0, 4, down_tile, 0)
    pl.semaphore_signal(free_act, inc=1, device_id=links.sibling, device_id_type=MESH)
    serve("down")

    pl.semaphore_wait(free_act, 1)

    def rows_half(first):
        return pl.ds(pl.multiple_of(first, 128), HALF)

    def gelu_tile(j, _):
        cols = pl.ds(pl.multiple_of(j * 768, 768), 768)
        low = (nt(branch[...], wdn[cols, :]) * pre[:, cols].astype(F32)).astype(BF)
        pre[:, cols] = low
        vec[pl.ds(VEC["up"] + j, 1), :] = jnp.sum(low.astype(F32), 0, keepdims=True)
        send[:, cols] = tn(flow[:, rows_half(other_half)], low).astype(BF)
        sum_up.tile_copy(send, j).start()
        sum_up.acc_tile(j)[...] = tn(flow[:, rows_half(own_half)], low).astype(BF)
        serve_at("gelu", j, (3,))
        return 0
    lax.fori_loop(0, 4, gelu_tile, 0)
    serve("up")

    dsec[...] += nt(pre[...], wup[...])
    serve("first")
    colsum[...] = jnp.zeros_like(colsum)

    def first_back(r, _):
        rows = pl.ds(pl.multiple_of(r * LN_ROWS, LN_ROWS), LN_ROWS)
        g = dsec[rows, :]
        n, rr = normalize(fsum[rows, :])
        colsum[0] += fold(g * n)
        colsum[1] += fold(g)
        df = norm_back(g * g1[...], n, rr)
        dsec[rows, :] = df
        low = df.astype(BF)
        branch[rows, :] = low
        colsum[2] += fold(low.astype(F32))
        return 0
    lax.fori_loop(0, QROWS // LN_ROWS, first_back, 0)
    for k, name in enumerate(("g1", "b1", "out")):
        vec[VEC[name]:VEC[name] + 1, :] = jnp.sum(colsum[k], 0, keepdims=True)
    serve("first_done")
    flow[...] = nt(branch[...], wo[...]).astype(BF)
    for t in reached:
        pl.semaphore_signal(free_pre, inc=1, device_id=t, device_id_type=MESH)
    pl.semaphore_wait(free_pre, len(reached))
    send[:, 3 * D:] = tn(ctx[:, rows_half(other_half)], branch[...]).astype(BF)
    out_copy = remote(send.at[:, pl.ds(3 * D, D)], pre.at[pl.ds(HALF, HALF), pl.ds(3 * D, D)],
                      sum_out.csend.at[0], sum_out.crecv.at[0], links.sibling)
    out_copy.start()
    sum_out.acc_tile(0)[...] = tn(ctx[:, rows_half(own_half)], branch[...]).astype(BF)
    serve("out")

    def attend_back(i, hp, nq):
        c0 = pl.multiple_of(hp * 128, 128)
        qs, ks, vs_ = (pl.ds(c0 + D * m, 128) for m in range(3))
        q, dc = queries_of(merged, i, qs, nq), queries_of(flow, i, pl.ds(c0, 128), nq)
        k, v = both(merged, i, ks), both(merged, i, vs_)
        live = key_live(i, nq)
        dq = dk = dv = None
        for h in range(2):
            kh = half(k, h)
            row = jnp.concatenate([lse[lse_row(i, hp * 2 + h, b), :] for b in range(nq // SLOTS)], 1)
            p = jnp.where(live, jnp.exp2(nt(kh, q) * (SCALE * LOG2E) - row), 0.0)
            dp = nt(half(v, h), dc)
            ds = (p * (dp - jnp.sum(p * dp, 0, keepdims=True))).astype(BF)
            a, b, c = nn(p.astype(BF), half(dc, h)), nn(ds, half(q, h)), tn(ds, kh)
            dv, dk, dq = (a, b, c) if h == 0 else (dv + a, dk + b, dq + c)
        dq, dk, dv = (dq * SCALE).astype(BF), (dk * SCALE).astype(BF), dv.astype(BF)
        for b in range(2):
            at = slice(b * SLOTS, (b + 1) * SLOTS)
            merged[rows_of(i + 4 * b), qs] = dq[at] if b * SLOTS < nq else jnp.zeros((SLOTS, 128), BF)
            merged[rows_of(i + 4 * b), ks] = dk[at]
            merged[rows_of(i + 4 * b), vs_] = dv[at]

    def weights_of(g):
        cols = [pl.ds(pl.multiple_of(m * D + g * 256, 256), 256) for m in range(3)]
        grads = jnp.concatenate([merged[:, c] for c in cols], 1)
        tile = pl.ds(pl.multiple_of(g * 768, 768), 768)
        send[:, tile] = tn(x[:, rows_half(other_half)], grads).astype(BF)
        for k in range(3):
            @pl.when(g == k)
            def _():
                sum_qkv[k].tile_copy(send, 0).start()
        pre[0:HALF, tile] = tn(x[:, rows_half(own_half)], grads).astype(BF)
        for m in (0, 2):
            sums = jnp.sum(merged[:, cols[m]].astype(F32), 0, keepdims=True)
            vec_qv[m // 2:m // 2 + 1, pl.ds(pl.multiple_of(g * 256, 256), 256)] = sums

    def group(g, _):
        def whole(i, _):
            for u in range(2):
                attend_back(i, g * 2 + u, 256)
            return 0
        lax.fori_loop(0, WHOLE, whole, 0)
        serve_at("mid", g, range(2))
        for u in range(2):
            attend_back(WHOLE, g * 2 + u, SLOTS)
        weights_of(g)
        serve_at("end", g, range(2))
        return 0
    lax.fori_loop(0, 2, group, 0)

    for i in range(4):
        y_local(i).wait()
    for i in range(3):
        y_remote(i).wait()

    def ig_remote(i):
        return remote(ogv.at[rows_of(i)], ig_ref.at[pair_of(i)], xs.at[i], xr.at[10 + i], partner)
    mid_recv = wo.at[pl.ds(0, SLOTS)]
    mid_copy = remote(ogv.at[rows_of(3)], mid_recv, xs.at[3], xr.at[13], partner)
    for u in (4, 5):
        attend_back(WHOLE, u, SLOTS)
    ogv[rows_of(3), :] = nt(merged[rows_of(7), :], wqkv[...]).astype(BF)
    mid_copy.start()

    def last_whole(i, _):
        for u in (4, 5):
            attend_back(i, u, 256)
        ogv[rows_of(i), :] = (nt(merged[rows_of(i + 4), :], wqkv[...]) + dsec[rows_of(i + 4), :]).astype(BF)
        ig_remote(i).start()
        return 0
    lax.fori_loop(0, WHOLE, last_whole, 0)
    serve("mid2")
    weights_of(2)
    serve("end2")

    g = nt(merged[0:OWN, :], wqkv[...]) + dsec[0:OWN, :]
    x[0:384, :] = g[0:384].astype(BF)
    dsec[0:SLOTS, :] = g[384:]

    def ig_local(i):
        return pltpu.make_async_copy(x.at[pl.ds(i * SLOTS, SLOTS)], ig_ref.at[pair_of(i)], iosem.at[i])
    for i in range(3):
        ig_local(i).start()
    mid_copy.wait()
    x[384:512, :] = (dsec[0:SLOTS, :] + mid_recv[...].astype(F32)).astype(BF)
    ig_local(3).start()
    for name in tail:
        serve(name)
    for i in range(4):
        ig_local(i).wait()
        if i < 3:
            ig_remote(i).wait()


def layer(*args):
    any_, vm, sm = (pl.BlockSpec(memory_space=m) for m in (pl.ANY, pltpu.VMEM, pltpu.SMEM))
    S, V, dma = jax.ShapeDtypeStruct, pltpu.VMEM, pltpu.SemaphoreType.DMA
    sems = sum_sems(4) + sum_sems(4) + sum_sems(1) + sum_sems(1) + sum_sems(1) + sum_sems(1)
    return pl.pallas_call(
        layer_kernel,
        out_shape=(S((7, SLOTS, D), BF), S((7, SLOTS, D), BF), S((D, FF), BF), S((D, FF), BF), S((D, D), BF),
                   S((3, D, D), BF), S((VROWS, D), F32), S((8, D), F32)),
        in_specs=[any_] * 2 + [sm] * 2 + [any_, vm, any_, vm, vm, vm, any_, vm, any_, vm, vm, vm],
        out_specs=(any_,) * 6 + (vm,) * 2,
        scratch_shapes=[
            V((KROWS, D), BF), V((KROWS, 3 * D), BF), V((QROWS, D), BF), V((QROWS, D), F32),
            V((QROWS, D), BF), V((QROWS, FF), BF), V((QROWS, FF), BF), V((QROWS, D), BF), V((QROWS, D), F32),
            V((D, 3 * D), BF), V((D, D), BF), V((D, FF), BF), V((FF, D), BF), V((QROWS, D), BF),
            V((HALF, FF), BF), V((D, FF), BF), V((RECV_ROWS, FF), BF), V((RECV_ROWS, FF), BF),
            V((1, 3 * D), F32), V((1, FF), F32), V((6, 1, D), F32), V((3, 8, D), F32), V((96, SLOTS), F32),
            dma((4,)), dma((8,)), dma((7,)), dma((14,)), pltpu.SemaphoreType.REGULAR, pltpu.SemaphoreType.REGULAR,
            dma((7,)), dma((7,)), dma((4,)), dma((4, 4))] + sems,
        compiler_params=pltpu.CompilerParams(collective_id=1, has_side_effects=True, vmem_limit_bytes=63 * 2**20),
    )(*args)


def widen_kernel(down_ref, up_ref, out_ref, qkv_ref, y_ref, ig_ref, vec, vec_qv, down_o, up_o, out_o, qkv_o, y_o, ig_o,
                 v_qv, v_out, v_g1, v_b1, v_up, v_down, v_g2, v_b2, buf, stage, rows, rsem, wsem, ysem):
    for k in range(2):
        v_qv[:, k * D:(k + 1) * D] = vec_qv[k:k + 1, :]
    for ref, name in ((v_out, "out"), (v_g1, "g1"), (v_b1, "b1"), (v_up, "up"), (v_down, "down"),
                      (v_g2, "g2"), (v_b2, "b2")):
        for k in range(ref.shape[1] // D):
            ref[:, k * D:(k + 1) * D] = vec[VEC[name] + k:VEC[name] + k + 1, :]
    tiles = []
    for t in range(4):
        tiles.append((down_ref.at[:, pl.ds(t * D, D)], [(down_o.at[0, pl.ds(t * D, D), :], 0, D)]))
    for t in range(4):
        tiles.append((up_ref.at[:, pl.ds(t * D, D)], [(up_o.at[0, :, pl.ds(t * D, D)], 0, D)]))
    tiles.append((out_ref, [(out_o.at[0], 0, D)]))
    for t in range(3):
        tiles.append((qkv_ref.at[t], [(qkv_o.at[0, :, pl.ds(m * D + t * 256, 256)], m * 256, 256) for m in range(3)]))
    n = len(tiles)

    def read(t):
        return pltpu.make_async_copy(tiles[t][0], buf.at[t % 4], rsem.at[t % 4])

    def writes(t):
        return [pltpu.make_async_copy(stage.at[t % 3, :, pl.ds(c, w)], to, wsem.at[t % 3, m])
                for m, (to, c, w) in enumerate(tiles[t][1])]

    def rows_in(k):
        return pltpu.make_async_copy((y_ref, ig_ref)[k], rows.at[k], ysem.at[k])

    def rows_out(k):
        return pltpu.make_async_copy(rows.at[k], (y_o, ig_o)[k], ysem.at[k])
    for t in range(3):
        read(t).start()
    for k in range(2):
        rows_in(k).start()
    for t in range(n):
        if t + 3 < n:
            read(t + 3).start()
        read(t).wait()
        if t >= 3:
            for w in writes(t - 3):
                w.wait()

        def chunk(r, _):
            part = pl.ds(pl.multiple_of(r * 64, 64), 64)
            stage[t % 3, part, :] = buf[t % 4, part, :].astype(F32)
            return 0
        lax.fori_loop(0, D // 64, chunk, 0)
        for w in writes(t):
            w.start()
        if t == 2:
            for k in range(2):
                rows_in(k).wait()
                rows_out(k).start()
    for t in range(n - 3, n):
        for w in writes(t):
            w.wait()
    for k in range(2):
        rows_out(k).wait()


def widen(*args):
    S, dma = jax.ShapeDtypeStruct, pltpu.SemaphoreType.DMA
    hbm, vm = pl.BlockSpec(memory_space=pltpu.HBM), pl.BlockSpec(memory_space=pltpu.VMEM)
    rows = S((7, SLOTS, D), BF)
    vectors = tuple(S((1, n), F32) for n in (2 * D, D, D, D, FF, D, D, D))
    return pl.pallas_call(
        widen_kernel,
        out_shape=(S((1, FF, D), F32), S((1, D, FF), F32), S((1, D, D), F32), S((1, D, 3 * D), F32), rows, rows) + vectors,
        in_specs=[hbm] * 6 + [vm] * 2, out_specs=(hbm,) * 6 + (vm,) * 8,
        scratch_shapes=[pltpu.VMEM((4, D, D), BF), pltpu.VMEM((3, D, D), F32), pltpu.VMEM((2, 7, SLOTS, D), BF),
                        dma((4,)), dma((3, 3)), dma((2,))],
        compiler_params=pltpu.CompilerParams(vmem_limit_bytes=63 * 2**20),
    )(*args)


def body(hidden, text_counts, region_counts, qkv_weight, qv_bias, out_weight, out_bias, norm1_gain, norm1_bias,
         up_weight, up_bias, down_weight, down_bias, norm2_gain, norm2_bias, out_grad):
    y, ig, down, up, out, qkv, vec, vec_qv = layer(
        hidden[:, 0], out_grad[:, 0], text_counts, region_counts, qkv_weight[0], qv_bias, out_weight[0], out_bias,
        norm1_gain, norm1_bias, up_weight[0], up_bias, down_weight[0], down_bias, norm2_gain, norm2_bias)
    down, up, out, qkv, y, ig, v_qv, v_out, v_g1, v_b1, v_up, v_down, v_g2, v_b2 = widen(down, up, out, qkv, y, ig, vec, vec_qv)
    return y[:, None], ig[:, None], qkv, v_qv, out, v_out, v_g1, v_b1, up, v_up, down, v_down, v_g2, v_b2


def solution(mesh):
    rows, pairs, whole = P("batch", "mod", None, None), P("batch"), P()
    return jax.shard_map(body, mesh=mesh, in_specs=(rows, pairs, pairs) + (whole,) * 12 + (rows,),
                         out_specs=(rows, rows) + (whole,) * 12, check_vma=False)
```

```python
import functools
import math

import jax
import jax.numpy as jnp
from jax import lax
from jax.experimental import pallas as pl
from jax.experimental.pallas import tpu as pltpu
from jax.sharding import PartitionSpec as P

MESH = pl.DeviceIdType.MESH
BF, F32 = jnp.bfloat16, jnp.float32
D, FF, SLOTS = 768, 3072, 128
WHOLE = 3
OWN = (WHOLE + 1) * SLOTS
QROWS = OWN + WHOLE * SLOTS
KROWS = 2 * OWN
HALF = D // 2
EPS = 1e-6
MASKED = -1e9
LOG2E = math.log2(math.e)
SCALE = 0.125
LN_ROWS = 128
PARTS = 6
CUTS = (192, 96, 48)
RECV_AT = (0, 192, 288, 336, 384, 432)
RECV_ROWS = 480
QUARTER = HALF // 4
VEC = dict(out=0, g1=1, b1=2, up=3, down=7, g2=8, b2=9)
VROWS = 16


def nn(a, b):
    return lax.dot_general(a, b, (((1,), (0,)), ((), ())), preferred_element_type=F32)


def nt(a, b):
    return lax.dot_general(a, b, (((1,), (1,)), ((), ())), preferred_element_type=F32)


def tn(a, b):
    return lax.dot_general(a, b, (((0,), (0,)), ((), ())), preferred_element_type=F32)


def gelu_pair(v):
    e = jnp.exp2(v * v * (-0.5 * LOG2E))
    d = 1.0 + (0.3275911 / math.sqrt(2.0)) * jnp.abs(v)
    t = pl.reciprocal(d, approx=True)
    t = t * (2.0 - d * t)
    poly = 0.5 * 1.061405429 * t - 0.5 * 1.453152027
    poly = ((poly * t + 0.5 * 1.421413741) * t - 0.5 * 0.284496736) * t + 0.5 * 0.254829592
    tail = poly * t * e
    cdf = jnp.where(v >= 0, 1.0 - tail, tail)
    return v * cdf, cdf + v * e * (1.0 / math.sqrt(2.0 * math.pi))


def normalize(s):
    centre = s - jnp.mean(s, -1, keepdims=True)
    r = lax.rsqrt(jnp.mean(centre * centre, -1, keepdims=True) + EPS)
    return centre * r, r


def norm_back(g, n, r):
    return r * (g - jnp.mean(g, -1, keepdims=True) - n * jnp.mean(g * n, -1, keepdims=True))


def fold(v):
    return v.reshape(v.shape[0] // 8, 8, v.shape[1]).sum(0)


def half(v, h):
    lane = lax.broadcasted_iota(jnp.int32, v.shape, 1)
    return jnp.where((lane < 64) if h == 0 else (lane >= 64), v, jnp.zeros((), BF))


def place():
    mod, batch = lax.axis_index("mod"), lax.axis_index("batch")
    return mod * 2 + lax.rem(batch // 2, 2), batch // 16, lax.rem(batch // 4, 4), lax.rem(batch, 2)


def device(x, y, z, core):
    return (x // 2, y * 16 + z * 4 + lax.rem(x, 2) * 2 + core)


def near(v):
    return v + 1 - 2 * lax.rem(v, 2)


def remote(src, dst, send, recv, target):
    return pltpu.make_async_remote_copy(src, dst, send, recv, device_id=target, device_id_type=MESH)


class Links:
    def __init__(self):
        x, y, z, core = place()
        self.targets = [device(near(x), y, z, core), device(x, near(y), z, core), device(x, y, near(z), core),
                        device(3 - x, y, z, core), device(x, 3 - y, z, core), device(x, y, 3 - z, core)]
        bits = [lax.rem((v + 1) // 2, 2) for v in (x, y, z)] + [v // 2 for v in (x, y, z)]
        self.sibling, self.core = device(x, y, z, 1 - core), core
        self.coords = [x, y, z]
        self.across = [self.along(a, 2) for a in range(3)]
        self.bits = bits

    def along(self, axis, d):
        place_ = list(self.coords)
        place_[axis] = lax.rem(place_[axis] + d, 4)
        return device(*place_, self.core)


EVEN = [[(p + s) % 6 for s in range(6)] for p in range(6)]
SPARE_X = [[1, 2, 4, 5, 0, 3], [4, 5, 1, 2, 3, 0], [2, 4, 5, 1, 0, 3], [5, 1, 2, 4, 3, 0]]


class Sum:
    def __init__(self, links, width, routes, acc, core, recv, out, sems):
        self.links, self.routes, self.parts, self.part = links, routes, len(routes), width // len(routes)
        self.at, self.gone = [], []
        for route in routes:
            at, gone = [0], []
            for s, r in enumerate(CUTS):
                bit = links.bits[route[s]]
                gone.append(at[-1] + (1 - bit) * r)
                at.append(at[-1] + bit * r)
            self.at.append(at)
            self.gone.append(gone)
        self.acc_at, self.core_at, self.recv_at, self.out = acc, core, recv, out
        self.csend, self.crecv, self.ssend, self.srecv, self.gsend, self.grecv, self.fsend, self.frecv, self.local = sems

    def view(self, where, row, rows, col, cols):
        ref, r0, c0 = where
        if not isinstance(row, int):
            row = pl.multiple_of(row + r0, 16)
        else:
            row = row + r0
        return ref.at[pl.ds(row, rows), pl.ds(c0 + col, cols)]

    def tile_copy(self, send, t):
        c0 = self.core_at[2]
        cols = pl.ds(pl.multiple_of(c0 + t * 768, 128), 768)
        return remote(send.at[:, cols], self.core_at[0].at[pl.ds(self.core_at[1], HALF), cols],
                      self.csend.at[t], self.crecv.at[t], self.links.sibling)

    def acc_tile(self, t):
        ref, r0, c0 = self.acc_at
        return ref.at[pl.ds(r0, HALF), pl.ds(pl.multiple_of(c0 + t * 768, 128), 768)]

    def step_copy(self, p, s):
        col, w = p * self.part, self.part
        if s < 3:
            src = self.view(self.acc_at, self.gone[p][s], CUTS[s], col, w)
        else:
            src = self.view(self.acc_at, self.at[p][3], CUTS[2], col, w)
        dst = self.view(self.recv_at, RECV_AT[s], CUTS[min(s, 2)], col, w)
        return remote(src, dst, self.ssend.at[p], self.srecv.at[p, s], self.links.targets[self.routes[p][s]])

    def add(self, p, row, rows, src, src_row):
        a = self.view(self.acc_at, row, rows, p * self.part, self.part)
        b = self.view(src, src_row, rows, p * self.part, self.part)
        n = 48
        def chunk(i, _):
            rr = pl.ds(pl.multiple_of(i * n, 16), n)
            a[rr, :] = a[rr, :] + b[rr, :]
            return 0
        if rows == n:
            a[...] = a[...] + b[...]
        else:
            lax.fori_loop(0, rows // n, chunk, 0)

    def out_view(self, p, row, rows):
        start = pl.multiple_of(self.links.core * HALF + row, 16)
        return self.out.at[pl.ds(start, rows), pl.ds(p * self.part, self.part)]

    def place_copy(self, p):
        return pltpu.make_async_copy(self.view(self.acc_at, self.at[p][3], CUTS[2], p * self.part, self.part),
                                     self.out_view(p, self.at[p][3], CUTS[2]), self.local.at[p])

    def gather_copy(self, p, s):
        row = self.at[p][s + 1]
        dst = self.out_view(p, row, CUTS[s])
        src = self.view(self.acc_at, row, CUTS[s], p * self.part, self.part) if s == 2 else dst
        return remote(src, dst, self.gsend.at[p], self.grecv.at[p, s], self.links.targets[self.routes[p][s]])

    def pass_copy(self, p, k):
        if k == 3:
            dst = self.out_view(p, self.at[p][3], CUTS[2])
            src = self.view(self.acc_at, self.at[p][3], CUTS[2], p * self.part, self.part)
        else:
            src = dst = self.out_view(p, self.gone[p][k], CUTS[k])
        return remote(src, dst, self.fsend.at[p], self.frecv.at[p, k], self.links.sibling)

    count = 11

    def step(self, k, send):
        if k == 0:
            done = 0
            for p in range(self.parts):
                need = ((p + 1) * self.part - 1) // 768
                while done <= need:
                    self.tile_copy(send, done).wait()
                    done += 1
                self.add(p, 0, HALF, self.core_at, 0)
                self.step_copy(p, 0).start()
        elif k <= 6:
            s = k - 1
            for p in range(self.parts):
                self.step_copy(p, s).wait()
                self.add(p, self.at[p][min(s + 1, 3)], CUTS[min(s, 2)], self.recv_at, RECV_AT[s])
                if s < 5:
                    self.step_copy(p, s + 1).start()
                else:
                    self.place_copy(p).start()
                    self.gather_copy(p, 2).start()
                    self.pass_copy(p, 3).start()
        elif k <= 9:
            s = 9 - k
            for p in range(self.parts):
                if s == 2:
                    self.place_copy(p).wait()
                self.gather_copy(p, s).wait()
                if s > 0:
                    self.gather_copy(p, s - 1).start()
                self.pass_copy(p, s + 1).wait_send()
                self.pass_copy(p, s).start()
        else:
            for p in range(self.parts):
                self.pass_copy(p, 0).wait_send()
                for k in range(4):
                    self.pass_copy(p, k).wait_recv()


class VectorSum:
    count = 8

    def __init__(self, links, vec, slots, sems):
        self.links, self.vec, self.slots = links, vec, slots
        self.ssem, self.rsem = sems

    def copy(self, s):
        return remote(self.vec, self.slots.at[pl.ds(s * VROWS, VROWS)], self.ssem.at[s], self.rsem.at[s],
                      self.links.sibling if s == 0 else self.links.targets[s - 1])

    def step(self, k, send):
        if k > 0:
            self.copy(k - 1).wait()
            self.vec[...] = self.vec[...] + self.slots[(k - 1) * VROWS:k * VROWS, :]
        if k < 7:
            self.copy(k).start()


class AxisSum:
    count = 5

    def __init__(self, links, vec, slots, first, sems):
        self.links, self.vec, self.slots, self.first = links, vec, slots, first
        self.ssem, self.rsem = sems

    def slot(self, s, k):
        return self.slots.at[pl.ds(pl.multiple_of(self.first + (s * 4 + k) * 8, 8), 8)]

    def copy(self, s, d):
        if s == 0:
            return remote(self.vec, self.slot(0, 0), self.ssem.at[0], self.rsem.at[0, 0], self.links.sibling)
        return remote(self.vec, self.slot(s, self.links.coords[s - 1]), self.ssem.at[d], self.rsem.at[s, d],
                      self.links.along(s - 1, d))

    def step(self, k, send):
        if k == 1:
            self.copy(0, 0).wait()
            self.vec[...] = self.vec[...] + self.slot(0, 0)[...]
        elif k > 1:
            self.slot(k - 1, self.links.coords[k - 2])[...] = self.vec[...]
            for d in (1, 3, 2):
                self.copy(k - 1, d).wait()
            total = self.slot(k - 1, 0)[...]
            for i in range(1, 4):
                total = total + self.slot(k - 1, i)[...]
            self.vec[...] = total
        if k < 4:
            for d in (2, 1, 3) if k else (0,):
                self.copy(k, d).start()


def sum_sems(tiles):
    dma = pltpu.SemaphoreType.DMA
    return [dma((tiles,)), dma((tiles,)), dma((PARTS,)), dma((PARTS, 6)), dma((PARTS,)), dma((PARTS, 3)),
            dma((PARTS,)), dma((PARTS, 4)), dma((PARTS,))]


def layer_kernel(hid, og, tc, rc, wqkv_h, qvb, wo_h, bo_l, g1_l, b1_l, wup_h, bup_l, wdn_h, bdn_l, g2_l, b2_l,
                 y_ref, ig_ref, down_o, up_o, out_o, qkv_o, vec, vec_qv,
                 x, merged, ctx, fsum, flow, act, pre, branch, dsec, wqkv, wo, wup, wdn, ogv,
                 send, s1, s1recv, s2recv, bqkv, bup, small, colsum, lse, wsem, iosem, xs, xr, free_act, free_pre, vs, vr, qs_sem, qr_sem, *sems):
    mod, batch = lax.axis_index("mod"), lax.axis_index("batch")
    links = Links()
    partner = (1 - mod, batch)
    core = links.core
    barrier = pltpu.get_barrier_semaphore()
    reached = links.targets + links.across + [links.sibling]
    for t in reached:
        pl.semaphore_signal(barrier, inc=1, device_id=t, device_id_type=MESH)

    def pair_of(i):
        return i + mod * (6 - 2 * i)

    def given(i):
        return i + (1 - mod) * (6 - 2 * i)

    def own_count(i):
        return jnp.where(mod == 0, tc[pair_of(i)], rc[pair_of(i)])

    def other_count(i):
        return jnp.where(mod == 0, rc[pair_of(i)], tc[pair_of(i)])

    def rows_of(i, n=SLOTS):
        return pl.ds(pl.multiple_of(i * SLOTS, SLOTS), n)

    weights = [pltpu.make_async_copy(src, dst, wsem.at[k])
               for k, (src, dst) in enumerate([(wqkv_h, wqkv), (wo_h, wo), (wup_h, wup), (wdn_h, wdn)])]
    xin = [pltpu.make_async_copy(hid.at[pair_of(i)], x.at[rows_of(i)], iosem.at[i]) for i in range(4)]
    ogin = [pltpu.make_async_copy(og.at[pair_of(i)], ogv.at[rows_of(i)], iosem.at[4 + i]) for i in range(4)]
    for c in xin + weights[:1]:
        c.start()
    pl.semaphore_wait(barrier, len(reached))

    def x_copy(i):
        return remote(hid.at[given(i)], x.at[rows_of(i + 4)], xs.at[i], xr.at[i], partner)

    def og_copy(i):
        return remote(og.at[given(i)], ogv.at[rows_of(i + 4)], xs.at[4 + i], xr.at[4 + i], partner)
    for i in range(4):
        x_copy(i).start()
    for i in range(3):
        og_copy(i).start()
    for c in weights[1:] + ogin:
        c.start()

    bqkv[:, 0:768] = qvb[:, 0:768].astype(F32)
    bqkv[:, 768:1536] = jnp.zeros((1, 768), F32)
    bqkv[:, 1536:2304] = qvb[:, 768:1536].astype(F32)
    bup[...] = bup_l[...].astype(F32)
    for k, l in enumerate((bo_l, g1_l, b1_l, bdn_l, g2_l, b2_l)):
        small[k] = l[...].astype(F32)
    bo, g1, b1, bdn, g2, b2 = (small.at[k] for k in range(6))

    left = list(sems)

    def take(n):
        out = left[:n]
        del left[:n]
        return out
    sum_down = Sum(links, FF, SPARE_X, (s1, 0, 0), (s1, HALF, 0), (s1recv, 0, 0), down_o, take(9))
    sum_up = Sum(links, FF, EVEN, (act, 0, 0), (act, HALF, 0), (s2recv, 0, 0), up_o, take(9))
    sum_out = Sum(links, D, EVEN, (pre, 0, 3 * D), (pre, HALF, 3 * D), (wup, 0, 3 * D), out_o, take(9))
    recv = [(wup, 0, 0), (wup, 0, D), (wup, 0, 2 * D)]
    sum_qkv = [Sum(links, D, EVEN, (pre, 0, k * D), (pre, HALF, k * D), recv[k], qkv_o.at[k], take(9)) for k in range(3)]
    sum_vec = VectorSum(links, vec, fsum, (vs, vr))
    sum_qv = AxisSum(links, vec_qv, fsum, 7 * VROWS, (qs_sem, qr_sem))
    tail = ["tail" + str(k) for k in range(10)]
    ends = ["end0", "end1", "end2"]
    late = ["mid0", "end0", "mid1", "end1", "mid2", "end2"] + tail
    when = [(sum_qkv[2], late[5:]), (sum_qv, late[5:]), (sum_qkv[0], late[1:]), (sum_qkv[1], late[3:]),
            (sum_out, ["out"] + late), (sum_vec, ["out"] + late),
            (sum_down, ["down", "gelu3", "first", "out"] + ends + tail[1::2]), (sum_up, ["up", "out"] + ends + [tail[k] for k in (0, 2, 4, 6, 8, 9)])]

    plan = {}
    for s, places in when:
        for k in range(s.count):
            plan.setdefault(places[k], []).append((s, k))

    def serve(name):
        for s, k in plan.get(name, []):
            s.step(k, send)

    def serve_at(name, t, values):
        for k in values:
            @pl.when(t == k)
            def _():
                serve(name + str(k))

    own_half, other_half = core * HALF, (1 - core) * HALF

    for c in xin + weights[:1]:
        c.wait()

    def project(first, n):
        def tile(j, _):
            cols = pl.ds(pl.multiple_of(j * 768, 768), 768)
            merged[first, cols] = (nn(x[first, :], wqkv[:, cols]) + bqkv[:, cols]).astype(BF)
            return 0
        lax.fori_loop(0, 3, tile, 0)
    project(pl.ds(0, OWN), OWN)

    def key_live(i, nq):
        r = lax.broadcasted_iota(jnp.int32, (256, nq), 0)
        return r < jnp.where(r < SLOTS, own_count(i), SLOTS + other_count(i))

    def both(ref, i, cols):
        return jnp.concatenate([ref[rows_of(i), cols], ref[rows_of(i + 4), cols]], 0)

    def queries_of(ref, i, cols, nq):
        return both(ref, i, cols) if nq == 256 else ref[rows_of(i), cols]

    def lse_row(i, head, b):
        return pl.ds((i * 12 + head) * 2 + b, 1)

    def attend(i, hp, nq):
        c0 = hp * 128
        q = queries_of(merged, i, pl.ds(c0, 128), nq)
        k = both(merged, i, pl.ds(c0 + D, 128))
        v = both(merged, i, pl.ds(c0 + 2 * D, 128))
        live = key_live(i, nq)
        out = None
        for h in range(2):
            s = jnp.where(live, nt(half(k, h), q) * (SCALE * LOG2E), MASKED)
            top = jnp.max(s, 0, keepdims=True)
            e = jnp.exp2(s - top)
            total = jnp.sum(e, 0, keepdims=True)
            row = top + jnp.log2(total)
            for b in range(nq // SLOTS):
                lse[lse_row(i, hp * 2 + h, b), :] = row[:, b * SLOTS:(b + 1) * SLOTS]
            o = tn((e * (1.0 / total)).astype(BF), half(v, h))
            out = o if h == 0 else out + o
        for b in range(nq // SLOTS):
            ctx[rows_of(i + 4 * b), pl.ds(c0, 128)] = out[b * SLOTS:(b + 1) * SLOTS].astype(BF)

    def forward_pair(i, nq):
        x_copy(i).wait_recv()
        project(rows_of(i + 4), SLOTS)
        for hp in range(6):
            attend(i, hp, nq)

    def forward_whole(i, _):
        forward_pair(i, 256)
        return 0
    lax.fori_loop(0, WHOLE, forward_whole, 0)
    forward_pair(WHOLE, SLOTS)

    weights[1].wait()
    fsum[...] = x[0:QROWS, :].astype(F32) + nn(ctx[...], wo[...]) + bo[...]

    def first_rows(r, _):
        rows = pl.ds(pl.multiple_of(r * LN_ROWS, LN_ROWS), LN_ROWS)
        n, _r = normalize(fsum[rows, :])
        flow[rows, :] = (n * g1[...] + b1[...]).astype(BF)
        return 0
    lax.fori_loop(0, QROWS // LN_ROWS, first_rows, 0)

    weights[2].wait()

    def up_tile(j, _):
        cols = pl.ds(pl.multiple_of(j * 768, 768), 768)
        a, d = gelu_pair(nn(flow[...], wup[:, cols]) + bup[:, cols])
        act[:, cols] = a.astype(BF)
        pre[:, cols] = d.astype(BF)
        return 0
    lax.fori_loop(0, 4, up_tile, 0)
    weights[3].wait()
    dsec[...] = nn(act[...], wdn[...]) + bdn[...]
    for c in ogin:
        c.wait()
    for i in range(3):
        og_copy(i).wait()
    for i in range(4):
        x_copy(i).wait_send()

    vec[...] = jnp.zeros_like(vec)
    vec_qv[...] = jnp.zeros_like(vec_qv)
    colsum[...] = jnp.zeros_like(colsum)

    counts = [own_count(i) for i in range(4)] + [other_count(i) for i in range(3)]

    def second_rows(r, _):
        rows = pl.ds(pl.multiple_of(r * LN_ROWS, LN_ROWS), LN_ROWS)
        place_ = lax.broadcasted_iota(jnp.int32, (LN_ROWS, 1), 0) + r * LN_ROWS
        live = jnp.zeros((LN_ROWS, 1), F32)
        for k, count in enumerate(counts):
            live = jnp.where((place_ >= k * SLOTS) & (place_ < k * SLOTS + count), 1.0, live)
        n, rr = normalize(fsum[rows, :])
        n, rr = normalize(n * g1[...] + b1[...] + dsec[rows, :])
        dout = ogv[rows, :].astype(F32) * live
        ogv[rows, :] = ((n * g2[...] + b2[...]) * live).astype(BF)
        colsum[0] += fold(dout * n)
        colsum[1] += fold(dout)
        ds = norm_back(dout * g2[...], n, rr)
        dsec[rows, :] = ds
        low = ds.astype(BF)
        branch[rows, :] = low
        colsum[2] += fold(low.astype(F32))
        return 0
    lax.fori_loop(0, QROWS // LN_ROWS, second_rows, 0)
    for k, name in enumerate(("g2", "b2", "down")):
        vec[VEC[name]:VEC[name] + 1, :] = jnp.sum(colsum[k], 0, keepdims=True)

    def y_local(i):
        return pltpu.make_async_copy(ogv.at[rows_of(i)], y_ref.at[pair_of(i)], iosem.at[i])

    def y_remote(i):
        return remote(ogv.at[rows_of(i + 4)], y_ref.at[pair_of(i)], xs.at[i], xr.at[7 + i], partner)
    for i in range(4):
        y_local(i).start()
    for i in range(3):
        y_remote(i).start()

    def down_tile(t, _):
        def rows(first):
            return pl.ds(pl.multiple_of(t * 768 + first, 128), HALF)
        cols = pl.ds(pl.multiple_of(t * 768, 768), 768)
        send[:, cols] = tn(act[:, rows(other_half)], branch[...]).astype(BF)
        sum_down.tile_copy(send, t).start()
        sum_down.acc_tile(t)[...] = tn(act[:, rows(own_half)], branch[...]).astype(BF)
        return 0
    lax.fori_loop(0, 4, down_tile, 0)
    pl.semaphore_signal(free_act, inc=1, device_id=links.sibling, device_id_type=MESH)
    serve("down")

    pl.semaphore_wait(free_act, 1)

    def rows_half(first):
        return pl.ds(pl.multiple_of(first, 128), HALF)

    def gelu_tile(j, _):
        cols = pl.ds(pl.multiple_of(j * 768, 768), 768)
        low = (nt(branch[...], wdn[cols, :]) * pre[:, cols].astype(F32)).astype(BF)
        pre[:, cols] = low
        vec[pl.ds(VEC["up"] + j, 1), :] = jnp.sum(low.astype(F32), 0, keepdims=True)
        send[:, cols] = tn(flow[:, rows_half(other_half)], low).astype(BF)
        sum_up.tile_copy(send, j).start()
        sum_up.acc_tile(j)[...] = tn(flow[:, rows_half(own_half)], low).astype(BF)
        serve_at("gelu", j, (3,))
        return 0
    lax.fori_loop(0, 4, gelu_tile, 0)
    serve("up")

    dsec[...] += nt(pre[...], wup[...])
    serve("first")
    colsum[...] = jnp.zeros_like(colsum)

    def first_back(r, _):
        rows = pl.ds(pl.multiple_of(r * LN_ROWS, LN_ROWS), LN_ROWS)
        g = dsec[rows, :]
        n, rr = normalize(fsum[rows, :])
        colsum[0] += fold(g * n)
        colsum[1] += fold(g)
        df = norm_back(g * g1[...], n, rr)
        dsec[rows, :] = df
        low = df.astype(BF)
        branch[rows, :] = low
        colsum[2] += fold(low.astype(F32))
        return 0
    lax.fori_loop(0, QROWS // LN_ROWS, first_back, 0)
    for t in reached:
        pl.semaphore_signal(free_pre, inc=1, device_id=t, device_id_type=MESH)
    for k, name in enumerate(("g1", "b1", "out")):
        vec[VEC[name]:VEC[name] + 1, :] = jnp.sum(colsum[k], 0, keepdims=True)
    serve("first_done")
    flow[...] = nt(branch[...], wo[...]).astype(BF)
    send[:, 3 * D:] = tn(ctx[:, rows_half(other_half)], branch[...]).astype(BF)
    out_copy = remote(send.at[:, pl.ds(3 * D, D)], pre.at[pl.ds(HALF, HALF), pl.ds(3 * D, D)],
                      sum_out.csend.at[0], sum_out.crecv.at[0], links.sibling)
    pl.semaphore_wait(free_pre, len(reached))
    out_copy.start()
    sum_out.acc_tile(0)[...] = tn(ctx[:, rows_half(own_half)], branch[...]).astype(BF)
    serve("out")

    def attend_back(i, hp, nq):
        c0 = pl.multiple_of(hp * 128, 128)
        qs, ks, vs_ = (pl.ds(c0 + D * m, 128) for m in range(3))
        q, dc = queries_of(merged, i, qs, nq), queries_of(flow, i, pl.ds(c0, 128), nq)
        k, v = both(merged, i, ks), both(merged, i, vs_)
        live = key_live(i, nq)
        dq = dk = dv = None
        for h in range(2):
            kh = half(k, h)
            row = jnp.concatenate([lse[lse_row(i, hp * 2 + h, b), :] for b in range(nq // SLOTS)], 1)
            p = jnp.where(live, jnp.exp2(nt(kh, q) * (SCALE * LOG2E) - row), 0.0)
            dp = nt(half(v, h), dc)
            ds = (p * (dp - jnp.sum(p * dp, 0, keepdims=True))).astype(BF)
            a, b, c = nn(p.astype(BF), half(dc, h)), nn(ds, half(q, h)), tn(ds, kh)
            dv, dk, dq = (a, b, c) if h == 0 else (dv + a, dk + b, dq + c)
        dq, dk, dv = (dq * SCALE).astype(BF), (dk * SCALE).astype(BF), dv.astype(BF)
        for b in range(2):
            at = slice(b * SLOTS, (b + 1) * SLOTS)
            merged[rows_of(i + 4 * b), qs] = dq[at] if b * SLOTS < nq else jnp.zeros((SLOTS, 128), BF)
            merged[rows_of(i + 4 * b), ks] = dk[at]
            merged[rows_of(i + 4 * b), vs_] = dv[at]

    def weights_of(g):
        cols = [pl.ds(pl.multiple_of(m * D + g * 256, 256), 256) for m in range(3)]
        grads = jnp.concatenate([merged[:, c] for c in cols], 1)
        tile = pl.ds(pl.multiple_of(g * 768, 768), 768)
        send[:, tile] = tn(x[:, rows_half(other_half)], grads).astype(BF)
        for k in range(3):
            @pl.when(g == k)
            def _():
                sum_qkv[k].tile_copy(send, 0).start()
        pre[0:HALF, tile] = tn(x[:, rows_half(own_half)], grads).astype(BF)
        for m in (0, 2):
            sums = jnp.sum(merged[:, cols[m]].astype(F32), 0, keepdims=True)
            vec_qv[m // 2:m // 2 + 1, pl.ds(pl.multiple_of(g * 256, 256), 256)] = sums

    def group(g, _):
        def whole(i, _):
            for u in range(2):
                attend_back(i, g * 2 + u, 256)
            return 0
        lax.fori_loop(0, WHOLE, whole, 0)
        serve_at("mid", g, range(2))
        for u in range(2):
            attend_back(WHOLE, g * 2 + u, SLOTS)
        weights_of(g)
        serve_at("end", g, range(2))
        return 0
    lax.fori_loop(0, 2, group, 0)

    for i in range(4):
        y_local(i).wait()
    for i in range(3):
        y_remote(i).wait()

    def ig_remote(i):
        return remote(ogv.at[rows_of(i)], ig_ref.at[pair_of(i)], xs.at[i], xr.at[10 + i], partner)
    mid_recv = wdn.at[pl.ds(0, SLOTS)]
    mid_copy = remote(ogv.at[rows_of(3)], mid_recv, xs.at[3], xr.at[13], partner)
    for u in (4, 5):
        attend_back(WHOLE, u, SLOTS)
    ogv[rows_of(3), :] = nt(merged[rows_of(7), :], wqkv[...]).astype(BF)
    mid_copy.start()

    def last_whole(i, _):
        for u in (4, 5):
            attend_back(i, u, 256)
        ogv[rows_of(i), :] = (nt(merged[rows_of(i + 4), :], wqkv[...]) + dsec[rows_of(i + 4), :]).astype(BF)
        ig_remote(i).start()
        return 0
    lax.fori_loop(0, WHOLE, last_whole, 0)
    serve("mid2")
    weights_of(2)
    serve("end2")

    g = nt(merged[0:OWN, :], wqkv[...]) + dsec[0:OWN, :]
    x[0:384, :] = g[0:384].astype(BF)
    dsec[0:SLOTS, :] = g[384:]

    def ig_local(i):
        return pltpu.make_async_copy(x.at[pl.ds(i * SLOTS, SLOTS)], ig_ref.at[pair_of(i)], iosem.at[i])
    for i in range(3):
        ig_local(i).start()
    mid_copy.wait()
    x[384:512, :] = (dsec[0:SLOTS, :] + mid_recv[...].astype(F32)).astype(BF)
    ig_local(3).start()
    for name in tail:
        serve(name)
    for i in range(4):
        ig_local(i).wait()
        if i < 3:
            ig_remote(i).wait()


def layer(*args):
    any_, vm, sm = (pl.BlockSpec(memory_space=m) for m in (pl.ANY, pltpu.VMEM, pltpu.SMEM))
    S, V, dma = jax.ShapeDtypeStruct, pltpu.VMEM, pltpu.SemaphoreType.DMA
    sems = sum_sems(4) + sum_sems(4) + sum_sems(1) + sum_sems(1) + sum_sems(1) + sum_sems(1)
    return pl.pallas_call(
        layer_kernel,
        out_shape=(S((7, SLOTS, D), BF), S((7, SLOTS, D), BF), S((D, FF), BF), S((D, FF), BF), S((D, D), BF),
                   S((3, D, D), BF), S((VROWS, D), F32), S((8, D), F32)),
        in_specs=[any_] * 2 + [sm] * 2 + [any_, vm, any_, vm, vm, vm, any_, vm, any_, vm, vm, vm],
        out_specs=(any_,) * 6 + (vm,) * 2,
        scratch_shapes=[
            V((KROWS, D), BF), V((KROWS, 3 * D), BF), V((QROWS, D), BF), V((QROWS, D), F32),
            V((QROWS, D), BF), V((QROWS, FF), BF), V((QROWS, FF), BF), V((QROWS, D), BF), V((QROWS, D), F32),
            V((D, 3 * D), BF), V((D, D), BF), V((D, FF), BF), V((FF, D), BF), V((QROWS, D), BF),
            V((HALF, FF), BF), V((D, FF), BF), V((RECV_ROWS, FF), BF), V((RECV_ROWS, FF), BF),
            V((1, 3 * D), F32), V((1, FF), F32), V((6, 1, D), F32), V((3, 8, D), F32), V((96, SLOTS), F32),
            dma((4,)), dma((8,)), dma((7,)), dma((14,)), pltpu.SemaphoreType.REGULAR, pltpu.SemaphoreType.REGULAR,
            dma((7,)), dma((7,)), dma((4,)), dma((4, 4))] + sems,
        compiler_params=pltpu.CompilerParams(collective_id=1, has_side_effects=True, vmem_limit_bytes=63 * 2**20),
    )(*args)


def widen_kernel(down_ref, up_ref, out_ref, qkv_ref, y_ref, ig_ref, vec, vec_qv, down_o, up_o, out_o, qkv_o, y_o, ig_o,
                 v_qv, v_out, v_g1, v_b1, v_up, v_down, v_g2, v_b2, buf, stage, rows, rsem, wsem, ysem):
    for k in range(2):
        v_qv[:, k * D:(k + 1) * D] = vec_qv[k:k + 1, :]
    for ref, name in ((v_out, "out"), (v_g1, "g1"), (v_b1, "b1"), (v_up, "up"), (v_down, "down"),
                      (v_g2, "g2"), (v_b2, "b2")):
        for k in range(ref.shape[1] // D):
            ref[:, k * D:(k + 1) * D] = vec[VEC[name] + k:VEC[name] + k + 1, :]
    tiles = []
    for t in range(4):
        tiles.append((down_ref.at[:, pl.ds(t * D, D)], [(down_o.at[0, pl.ds(t * D, D), :], 0, D)]))
    for t in range(4):
        tiles.append((up_ref.at[:, pl.ds(t * D, D)], [(up_o.at[0, :, pl.ds(t * D, D)], 0, D)]))
    tiles.append((out_ref, [(out_o.at[0], 0, D)]))
    for t in range(3):
        tiles.append((qkv_ref.at[t], [(qkv_o.at[0, :, pl.ds(m * D + t * 256, 256)], m * 256, 256) for m in range(3)]))
    n = len(tiles)

    def read(t):
        return pltpu.make_async_copy(tiles[t][0], buf.at[t % 6], rsem.at[t % 6])

    def writes(t):
        return [pltpu.make_async_copy(stage.at[t % 4, :, pl.ds(c, w)], to, wsem.at[t % 4, m])
                for m, (to, c, w) in enumerate(tiles[t][1])]

    def rows_in(k):
        return pltpu.make_async_copy((y_ref, ig_ref)[k], rows.at[k], ysem.at[k])

    def rows_out(k):
        return pltpu.make_async_copy(rows.at[k], (y_o, ig_o)[k], ysem.at[k])
    for t in range(5):
        read(t).start()
    for k in range(2):
        rows_in(k).start()
    for t in range(n):
        if t + 5 < n:
            read(t + 5).start()
        read(t).wait()
        if t >= 4:
            for w in writes(t - 4):
                w.wait()

        def chunk(r, _):
            part = pl.ds(pl.multiple_of(r * 128, 128), 128)
            stage[t % 4, part, :] = buf[t % 6, part, :].astype(F32)
            return 0
        lax.fori_loop(0, D // 128, chunk, 0)
        for w in writes(t):
            w.start()
        if t == 2:
            for k in range(2):
                rows_in(k).wait()
                rows_out(k).start()
    for t in range(n - 4, n):
        for w in writes(t):
            w.wait()
    for k in range(2):
        rows_out(k).wait()


def widen(*args):
    S, dma = jax.ShapeDtypeStruct, pltpu.SemaphoreType.DMA
    hbm, vm = pl.BlockSpec(memory_space=pltpu.HBM), pl.BlockSpec(memory_space=pltpu.VMEM)
    rows = S((7, SLOTS, D), BF)
    vectors = tuple(S((1, n), F32) for n in (2 * D, D, D, D, FF, D, D, D))
    return pl.pallas_call(
        widen_kernel,
        out_shape=(S((1, FF, D), F32), S((1, D, FF), F32), S((1, D, D), F32), S((1, D, 3 * D), F32), rows, rows) + vectors,
        in_specs=[hbm] * 6 + [vm] * 2, out_specs=(hbm,) * 6 + (vm,) * 8,
        scratch_shapes=[pltpu.VMEM((6, D, D), BF), pltpu.VMEM((4, D, D), F32), pltpu.VMEM((2, 7, SLOTS, D), BF),
                        dma((6,)), dma((4, 3)), dma((2,))],
        compiler_params=pltpu.CompilerParams(vmem_limit_bytes=63 * 2**20),
    )(*args)


def body(hidden, text_counts, region_counts, qkv_weight, qv_bias, out_weight, out_bias, norm1_gain, norm1_bias,
         up_weight, up_bias, down_weight, down_bias, norm2_gain, norm2_bias, out_grad):
    y, ig, down, up, out, qkv, vec, vec_qv = layer(
        hidden[:, 0], out_grad[:, 0], text_counts, region_counts, qkv_weight[0], qv_bias, out_weight[0], out_bias,
        norm1_gain, norm1_bias, up_weight[0], up_bias, down_weight[0], down_bias, norm2_gain, norm2_bias)
    down, up, out, qkv, y, ig, v_qv, v_out, v_g1, v_b1, v_up, v_down, v_g2, v_b2 = widen(down, up, out, qkv, y, ig, vec, vec_qv)
    return y[:, None], ig[:, None], qkv, v_qv, out, v_out, v_g1, v_b1, up, v_up, down, v_down, v_g2, v_b2


def solution(mesh):
    rows, pairs, whole = P("batch", "mod", None, None), P("batch"), P()
    return jax.shard_map(body, mesh=mesh, in_specs=(rows, pairs, pairs) + (whole,) * 12 + (rows,),
                         out_specs=(rows, rows) + (whole,) * 12, check_vma=False)
```
